256 devices in a mesh: sect: 2 (over z_lo), grp: 64 (over y, z_hi, x), tp: 2 (over core).
Axes of the slice: x: 4, y: 4, z: 8 (z_hi: 4, z_lo: 2; z = z_hi * 2 + z_lo), core: 2. Of those that a mesh axis runs over, the one named last changes fastest.
Arguments:
- queries: bfloat16 [2, 512, 128, 576], P('sect', 'grp', 'tp'), may hold values from -11 to 11
- latent_rotary_cache: bfloat16 [2, 512, 512, 576], P('sect', 'grp'), may hold values from -4 to 4
- lengths: int32 [2, 512], P('sect', 'grp'), may hold values from 2 to 512, as said below
- section_hidden_rows: bfloat16 [2, 512, 7168], P('sect', 'grp', 'tp'), may hold values from -6 to 6
- row_expert_index: int32 [2, 512, 8], P('sect', 'grp'), may hold values from 0 to 15, all different within a row; in each aligned block of 8 rows (0 to 7, 8 to 15, ..., all dimensions but the last counted through in order) at most 8 rows name the same one
- routing_gate_weight: float32 [2, 512, 8], P('sect', 'grp'), may hold values from 0.05 to 0.5
- gate_matrix: bfloat16 [2, 7168, 16384], P('sect', 'tp', 'grp'), may hold values from -0.0625 to 0.0625
- up_weight: bfloat16 [2, 7168, 16384], P('sect', 'tp', 'grp'), may hold values from -0.0625 to 0.0625
- down_weight: bfloat16 [2, 16384, 7168], P('sect', 'grp', 'tp'), may hold values from -0.1875 to 0.1875
- adapter_input_factor: bfloat16 [2, 2, 3584, 512], P('sect', 'tp', 'grp'), may hold values from -0.0625 to 0.0625
- adapter_output_factor: bfloat16 [2, 2, 3584, 256], P('sect', 'tp', 'grp'), may hold values from -1.5 to 1.5
- adapter_up_output: bfloat16 [2, 32, 16384], P('sect', None, 'grp'), may hold values from -1.5 to 1.5
- adapter_down_input: bfloat16 [2, 16, 16384], P('sect', None, 'grp'), may hold values from -0.1875 to 0.1875
Outputs:
- expert_out: bfloat16 [2, 512, 7168], P('sect', 'grp', 'tp')
- attention_out: bfloat16 [2, 512, 128, 512], P('sect', 'grp', 'tp')
The draws below stay inside these ranges and needn't reach their ends.
Inputs may be any that keep to these rules, and one draw needn't show every extreme that they name: `row_expert_index`: each row names 8 different experts. Within the rows of one attention pair (aligned blocks of 8 rows) no expert is named more than 8 times, and in some blocks one expert is named exactly 8 times. `lengths`: in every aligned block of 8 sequences one sequence has exactly 512 cached rows.
All inputs are finite; a program needn't handle non-finite values.
Results may differ from the reference program's by a relative error of at most 0.008.
Values may be sent and summed in bfloat16 or wider, within the bound.
A program may use at most 128 MiB of HBM per device.

```python
import math
import jax
import jax.numpy as jnp
import numpy as np
from jax import lax

MODEL_WIDTH = 7168
H = 128
LAT = 512
QK = 192
EXPERT_HIDDEN = 1024
ADAPTER_RANK = 16
SEQ_DEV = 8
LEN = 512
KD = 576
SEQS = 512
SECTION_EXPERTS = 16
TOP = 8
CAP = 8
N_SECT = 2
N_TP = 2


def draw_latent_rotary_cache(key, part):
    key = jax.random.fold_in(key, 7)
    values = jnp.clip(jax.random.normal(key, (N_SECT, SEQS, LEN, KD), jnp.float32), -4.0, 4.0)
    return values.astype(jnp.bfloat16)


def draw_queries(key, part):
    key = jax.random.fold_in(key, 11)
    first = jax.random.fold_in(key, 0)
    values = jnp.clip(jax.random.normal(first, (N_SECT, SEQS, H, KD), jnp.float32), -6.0, 6.0)
    return values.astype(jnp.bfloat16)


def draw_lengths(key, part):
    key = jax.random.fold_in(key, 13)
    first, second = jax.random.split(key)
    spans = jax.random.randint(first, (N_SECT, SEQS), 2, LEN + 1)
    longest = jax.random.randint(second, (N_SECT, SEQS // SEQ_DEV, 1), 0, SEQ_DEV)
    places = jnp.arange(SEQ_DEV, dtype=jnp.int32)
    marked = (places[None, None, :] == longest).reshape(N_SECT, SEQS)
    return jnp.where(marked, LEN, spans).astype(jnp.int32)


def block_scale(own_key, shape, pieces, low, largest):
    def one(dim, blocks):
        draws = jax.random.uniform(jax.random.fold_in(jax.random.fold_in(own_key, 6), dim), (blocks,), jnp.float32, low / len(pieces), largest / len(pieces))
        return jnp.repeat(jnp.exp(draws), shape[dim] // blocks).reshape((-1,) + (1,) * (len(shape) - dim - 1))

    loudness = one(*pieces[0])
    for cut in pieces[1:]:
        loudness = loudness * one(*cut)
    return loudness


def routed_block(key, own, number, rows, number_of, top, bound, lean):
    order = jax.random.permutation(key, number_of)
    crowded, common = portions_of(number_of, rows * top, bound, lean, True), portions_of(number_of, rows * top, bound, lean, False)
    places = jnp.arange(number_of)

    def named(sizes, rotation):
        used = int((sizes > 0).sum())
        fixed = max(1, used // 4)
        shifted = fixed + (places - fixed + rotation * (used - fixed)) % max(1, number_of - fixed)
        return jnp.zeros((number_of,), jnp.int32).at[order[jnp.where(places < fixed, places, shifted)]].set(jnp.asarray(sizes, jnp.int32))

    sizes = jnp.where(number % 4 == 0, named(crowded, number // 4), named(common, number - number // 4 - 1))
    mixed = jax.random.permutation(jax.random.fold_in(own, 3), number_of)
    source_of, receiver = mixed[0:number_of // 2 * 2:2], mixed[1:number_of // 2 * 2:2]
    room = jnp.minimum(sizes[source_of] - 1, bound - sizes[receiver]) // 2
    room = jnp.where((source_of == order[0]) | (receiver == order[0]) | (sizes[receiver] == 0), 0, jnp.maximum(room, 0))
    shifted = jax.random.randint(jax.random.fold_in(own, 4), (number_of // 2,), 0, 1 << 20) % (room + 1)
    sizes = sizes.at[source_of].add(-shifted).at[receiver].add(shifted)
    labels = jnp.searchsorted(jnp.cumsum(sizes), jnp.arange(rows * top), side="right").astype(jnp.int32)
    grid = labels.reshape(top, rows).T
    grid = grid[jax.random.permutation(jax.random.fold_in(own, 1), rows)]
    rotation = jax.random.randint(jax.random.fold_in(own, 2), (rows, 1), 0, top)
    return jnp.take_along_axis(grid, (jnp.arange(top)[None, :] + rotation) % top, axis=1)


def portions_of(amount, total, reach, skew, full):
    portions = [(1 << 20) // math.isqrt(standing ** skew) + 1 for standing in range(1, amount + 1)]
    largest = reach if full else min(reach, max(-(-total // amount), total * portions[0] // sum(portions)))
    least = 1 if total - largest >= amount - 1 else 0
    given, surplus = [largest] + [least] * (amount - 1), total - largest - least * (amount - 1)
    while surplus > 0:
        candidates = [i for i in range(1, amount) if given[i] < largest] or [i for i in range(1, amount) if given[i] < reach]
        mass, budget = sum([portions[i] for i in candidates]), surplus
        for i in candidates:
            addition = min(reach - given[i], max(1, budget * portions[i] // mass), surplus)
            given[i] = given[i] + addition
            surplus = surplus - addition
    return np.array(given)


def scatter_about(stream_key, extent, scale, limit, pieces=(), kind=jnp.bfloat16):
    drawn = scale * jax.random.normal(stream_key, extent, jnp.float32)
    if pieces:
        drawn = drawn * block_scale(stream_key, extent, pieces, -0.22, 0.18)
    return jnp.clip(drawn, -limit, limit).astype(kind)


def setup_inputs(seed: int = 0) -> dict:
    seeds = jax.random.split(jax.random.key(seed), 14)
    queries = draw_queries(jax.random.fold_in(seeds[13], 71), 0)
    latent_rotary_cache = draw_latent_rotary_cache(jax.random.fold_in(seeds[13], 71), 0)
    lengths = draw_lengths(jax.random.fold_in(seeds[13], 71), 0)
    section_hidden_rows = scatter_about(seeds[3], (N_SECT, SEQS, MODEL_WIDTH), 1.0, 6.0, ((0, 2), (1, 64), (2, 2)))
    row_expert_index_keys = jax.random.split(jax.random.fold_in(seeds[4], 1), N_SECT * SEQS // SEQ_DEV)
    row_expert_index_turns = jax.random.permutation(jax.random.fold_in(seeds[4], 3), N_SECT * SEQS // SEQ_DEV)
    row_expert_index = jax.vmap(lambda own, number: routed_block(jax.random.fold_in(seeds[4], 2), own, number, SEQ_DEV, SECTION_EXPERTS, TOP, CAP, 2))(row_expert_index_keys, row_expert_index_turns).reshape((N_SECT, SEQS, TOP))
    routing_gate_weight = jnp.clip(jnp.exp(math.log(0.5) - 2.3025851 * jax.random.uniform(seeds[5], (N_SECT, SEQS, TOP), jnp.float32) ** block_scale(seeds[5], (N_SECT, SEQS, TOP), ((0, 2), (1, 64)), -0.2, 0.2)), 0.05, 0.5)
    gate_matrix = scatter_about(seeds[6], (N_SECT, MODEL_WIDTH, SECTION_EXPERTS * EXPERT_HIDDEN), MODEL_WIDTH ** -0.5, 0.0625, ((0, 2), (1, 2), (2, 64)))
    up_weight = scatter_about(seeds[7], (N_SECT, MODEL_WIDTH, SECTION_EXPERTS * EXPERT_HIDDEN), MODEL_WIDTH ** -0.5, 0.0625, ((0, 2), (1, 2), (2, 64)))
    down_weight = scatter_about(seeds[8], (N_SECT, SECTION_EXPERTS * EXPERT_HIDDEN, MODEL_WIDTH), EXPERT_HIDDEN ** -0.5, 0.1875, ((0, 2), (1, 64), (2, 2)))
    adapter_input_factor = scatter_about(seeds[9], (N_SECT, N_TP, MODEL_WIDTH // N_TP, SECTION_EXPERTS * 2 * ADAPTER_RANK), MODEL_WIDTH ** -0.5, 0.0625, ((0, 2), (1, 2), (2, 64)))
    adapter_output_factor = scatter_about(seeds[10], (N_SECT, N_TP, MODEL_WIDTH // N_TP, SECTION_EXPERTS * ADAPTER_RANK), ADAPTER_RANK ** -0.5, 1.5, ((0, 2), (1, 2), (2, 64)))
    adapter_up_output = scatter_about(seeds[11], (N_SECT, 2 * ADAPTER_RANK, SECTION_EXPERTS * EXPERT_HIDDEN), ADAPTER_RANK ** -0.5, 1.5, ((0, 2), (2, 64)))
    adapter_down_input = scatter_about(seeds[12], (N_SECT, ADAPTER_RANK, SECTION_EXPERTS * EXPERT_HIDDEN), EXPERT_HIDDEN ** -0.5, 0.1875, ((0, 2), (2, 64)))
    return dict(queries=queries, latent_rotary_cache=latent_rotary_cache, lengths=lengths, section_hidden_rows=section_hidden_rows, row_expert_index=row_expert_index, routing_gate_weight=routing_gate_weight, gate_matrix=gate_matrix, up_weight=up_weight, down_weight=down_weight, adapter_input_factor=adapter_input_factor, adapter_output_factor=adapter_output_factor, adapter_up_output=adapter_up_output, adapter_down_input=adapter_down_input)


def attend_block(block):
    query, latent, length = block
    scores = jnp.einsum('shk,slk->shl', query.astype(jnp.float32), latent.astype(jnp.float32)) * (QK ** -0.5)
    position = jnp.arange(LEN, dtype=jnp.int32)
    valid = position[None, None, :] < length[:, None, None]
    scores = jnp.where(valid, scores, -jnp.inf)
    top = jnp.max(scores, axis=2, keepdims=True)
    weights = jnp.exp(scores - top)
    probs = (weights / jnp.sum(weights, axis=2, keepdims=True)).astype(jnp.bfloat16)
    values = latent[:, :, :LAT].astype(jnp.float32)
    return jnp.einsum('shl,slk->shk', probs.astype(jnp.float32), values).astype(jnp.bfloat16)


def routed_expert_layer(rows, ids, gates, gate_matrix, up_weight, down_weight, input_factor_pair, output_factor_pair, up_pair, down_pair):
    def step(total, expert):
        gate_w = lax.dynamic_slice_in_dim(gate_matrix, expert * EXPERT_HIDDEN, EXPERT_HIDDEN, 1)
        up_w = lax.dynamic_slice_in_dim(up_weight, expert * EXPERT_HIDDEN, EXPERT_HIDDEN, 1)
        down_w = lax.dynamic_slice_in_dim(down_weight, expert * EXPERT_HIDDEN, EXPERT_HIDDEN, 0)
        factor_in = lax.dynamic_index_in_dim(input_factor_pair, expert, 1, keepdims=False)
        factor_out = lax.dynamic_index_in_dim(output_factor_pair, expert, 1, keepdims=False)
        factor_up = lax.dynamic_slice_in_dim(up_pair, expert * EXPERT_HIDDEN, EXPERT_HIDDEN, 1)
        factor_down = lax.dynamic_slice_in_dim(down_pair, expert * EXPERT_HIDDEN, EXPERT_HIDDEN, 1)
        low = jnp.dot(rows, factor_in, preferred_element_type=jnp.float32).astype(jnp.bfloat16)
        gate = jnp.dot(rows, gate_w, preferred_element_type=jnp.float32) + jnp.dot(low[:, :ADAPTER_RANK], factor_up[:ADAPTER_RANK], preferred_element_type=jnp.float32)
        up = jnp.dot(rows, up_w, preferred_element_type=jnp.float32) + jnp.dot(low[:, ADAPTER_RANK:], factor_up[ADAPTER_RANK:], preferred_element_type=jnp.float32)
        hidden = (jax.nn.silu(gate) * up).astype(jnp.bfloat16)
        narrow = jnp.dot(hidden, factor_down.T, preferred_element_type=jnp.float32)
        result = jnp.dot(hidden, down_w, preferred_element_type=jnp.float32) + jnp.dot(narrow, factor_out.T.astype(jnp.float32), precision=lax.Precision.HIGHEST)
        share = jnp.sum(jnp.where(ids == expert, gates, jnp.zeros_like(gates)), axis=1)
        return total + share[:, None] * result, None

    start = jnp.zeros((rows.shape[0], MODEL_WIDTH), jnp.float32)
    total, unused = lax.scan(step, start, jnp.arange(SECTION_EXPERTS, dtype=jnp.int32))
    return total.astype(jnp.bfloat16)


def reference(queries, latent_rotary_cache, lengths, section_hidden_rows, row_expert_index, routing_gate_weight, gate_matrix, up_weight, down_weight, adapter_input_factor, adapter_output_factor, adapter_up_output, adapter_down_input):
    blocks = N_SECT * SEQS // SEQ_DEV
    query_blocks = queries.reshape(blocks, SEQ_DEV, H, KD)
    cache_blocks = latent_rotary_cache.reshape(blocks, SEQ_DEV, LEN, KD)
    length_blocks = lengths.reshape(blocks, SEQ_DEV)
    attended = lax.map(attend_block, (query_blocks, cache_blocks, length_blocks))
    attention_out = attended.reshape(N_SECT, SEQS, H, LAT)
    expert_results = []
    for micro_batch in range(N_SECT):
        partner_section = N_SECT - 1 - micro_batch
        input_factor_pair = adapter_input_factor[micro_batch].reshape(MODEL_WIDTH, SECTION_EXPERTS, 2 * ADAPTER_RANK)
        output_factor_pair = adapter_output_factor[micro_batch].reshape(MODEL_WIDTH, SECTION_EXPERTS, ADAPTER_RANK)
        expert_results.append(routed_expert_layer(section_hidden_rows[micro_batch], row_expert_index[micro_batch], routing_gate_weight[micro_batch], gate_matrix[partner_section], up_weight[partner_section], down_weight[partner_section], input_factor_pair, output_factor_pair, adapter_up_output[micro_batch], adapter_down_input[micro_batch]))
    return jnp.stack(expert_results), attention_out
```

```python
import jax
import jax.numpy as jnp
from jax import lax
from jax.experimental import pallas as pl
from jax.experimental.pallas import tpu as pltpu
from jax.sharding import PartitionSpec as P

LAT = 512
QK = 192
SEQ = 8
HEADS = 64
KD = 576
LEN = 512
HALF = 3584
QUARTER = HALF // 2
WIDE = HALF + 128
HID = 256
SLICE = 56
N_COPIES = 134
N_LOCAL = 17
BF = jnp.bfloat16
F32 = jnp.float32
MESH = pl.DeviceIdType.MESH

STEPS = (1, -1, 3, -3)
MIRROR = (1, 0, 3, 2)
CHAIN_SLOTS = ((0, 3), (1, 2))


def dot(a, b):
    return jnp.dot(a, b, preferred_element_type=F32)


def dot_nt(a, b):
    return lax.dot_general(a, b, (((1,), (1,)), ((), ())), preferred_element_type=F32)


def kernel(
    q_hbm,
    cache_hbm,
    len_hbm,
    rows_hbm,
    ids_hbm,
    gates_hbm,
    wg_hbm,
    wu_hbm,
    wd_hbm,
    ain_hbm,
    cout_hbm,
    bq_hbm,
    e_hbm,
    expert_hbm,
    att_hbm,
    unit,
    zbuf,
    x_ref,
    gu_own,
    gu_got,
    p_ref,
    ra,
    from_left,
    from_right,
    q_sum,
    ra2,
    from_left2,
    from_right2,
    z_send,
    z_got,
    out_buf,
    wg,
    wu,
    wd,
    ain,
    cout,
    bq_got,
    e_got,
    pieces,
    pieces_got,
    tx,
    t_ref,
    ct,
    bpad,
    epad,
    q_buf,
    cache,
    lens,
    ids,
    gates,
    att_buf,
    send_sem,
    recv_sem,
    local_sem,
):
    sect = lax.axis_index("sect")
    grp = lax.axis_index("grp")
    tp = lax.axis_index("tp")
    y = grp // 16
    zh = (grp // 4) % 4
    x = grp % 4
    z = zh * 2 + sect
    expert = grp // 4

    def plane(dy, dx):
        return (sect, ((y + dy) % 4) * 16 + zh * 4 + (x + dx) % 4, tp)

    def across(step, dy):
        target = (z + step + 8) % 8
        return (target % 2, ((y + dy) % 4) * 16 + (target // 2) * 4 + x, tp)

    other_core = (sect, grp, 1 - tp)
    partner = (1 - sect, grp, tp)
    count = [0]

    def remote(src, dst, device):
        i = count[0]
        count[0] += 1
        return pltpu.make_async_remote_copy(
            src_ref=src,
            dst_ref=dst,
            send_sem=send_sem.at[i],
            recv_sem=recv_sem.at[i],
            device_id=device,
            device_id_type=MESH,
        )

    local_count = [0]

    def local(src, dst):
        i = local_count[0]
        local_count[0] += 1
        copy = pltpu.make_async_copy(src, dst, local_sem.at[i])
        copy.start()
        return copy

    load_rows = local(rows_hbm.at[0], unit.at[:, pl.ds(0, HALF)])
    load_ids = local(ids_hbm.at[0], ids)
    load_gates = local(gates_hbm.at[0], gates)
    load_ain = local(ain_hbm.at[0, 0], ain)
    load_cout = local(cout_hbm.at[0, 0], cout)
    load_len = local(len_hbm, lens)
    load_q = local(q_hbm.at[0], q_buf)
    load_cache = local(cache_hbm.at[0], cache)
    load_wg = local(wg_hbm.at[0], wg)
    load_wu = local(wu_hbm.at[0], wu)
    load_wd = local(wd_hbm.at[0], wd)

    barrier = pltpu.get_barrier_semaphore()
    peers = [other_core, plane(1, 0), plane(-1 + 4, 0), plane(0, 1), plane(0, 3)]
    peers += [across(step, dy) for step in STEPS for dy in range(4)]
    for peer in peers:
        pl.semaphore_signal(barrier, inc=1, device_id=peer, device_id_type=MESH)

    load_ids.wait()
    load_gates.wait()
    lane8 = lax.broadcasted_iota(jnp.int32, (SEQ, 128), 1)
    named = lane8 % 32
    share = jnp.zeros((SEQ, 128), F32)
    for k in range(8):
        share += jnp.where(ids[:, k : k + 1] == named, gates[:, k : k + 1], 0.0)
    first = share.astype(BF).astype(F32)
    second = (share - first).astype(BF).astype(F32)
    third = share - first - second
    terms = jnp.where(lane8 < 32, first, jnp.where(lane8 < 64, second, third))
    load_rows.wait()
    unit[:, HALF:WIDE] = jnp.where(lane8 < 96, terms, 0.0).astype(BF)

    pl.semaphore_wait(barrier, len(peers))

    z_copies = [
        remote(unit, zbuf.at[MIRROR[slot]], across(STEPS[slot], 0)) for slot in range(4)
    ]
    for copy in z_copies:
        copy.start()
    bq_copy = remote(bq_hbm.at[0], bq_got, partner)
    e_copy = remote(e_hbm.at[0], e_got, partner)
    bq_copy.start()
    e_copy.start()

    load_ain.wait()
    load_cout.wait()
    lane56 = lax.broadcasted_iota(jnp.int32, (SLICE, 128), 1)
    shift = (y // 2) * 64
    mine = (lane56 >= shift) & (lane56 < shift + 64)
    place = lane56 % 64
    for e in range(16):
        a_tile = ain[:, 128 * (e // 4) : 128 * (e // 4) + 128].astype(F32)
        c_tile = cout[:, 128 * (e // 8) : 128 * (e // 8) + 128].astype(F32)
        a_at, c_at = 32 * (e % 4), 16 * (e % 8)

        def turned(tile, by):
            by = by % 128
            return tile if by == 0 else pltpu.roll(tile, by, 1)

        low = jnp.where(
            place < 32,
            turned(a_tile, -a_at),
            jnp.where(place < 48, turned(c_tile, 32 - c_at), turned(c_tile, 48 - c_at)),
        )
        low = jnp.where(lane56 < 64, low, 0.0)
        both = low + pltpu.roll(low, 64, 1)
        pieces[e] = jnp.where(mine, both, 0.0).astype(BF)
    piece_copies = []
    for step in STEPS:
        for dy in range(4):
            target = (z + step + 8) % 8
            aim = ((y + dy) % 4) * 4 + target // 2
            copy = remote(pieces.at[aim], pieces_got.at[y * 4 + zh], across(step, dy))
            copy.start()
            piece_copies.append(copy)

    def attend(first_seq, n):
        def one(s, carry):
            cached = cache[s]
            query = q_buf[s]
            scores = dot(query[:, :LAT], cached[:LAT]) + dot(query[:, LAT:], cached[LAT:])
            scores = scores * QK ** (-0.5)
            position = lax.broadcasted_iota(jnp.int32, (HEADS, LEN), 1)
            at = lax.broadcasted_iota(jnp.int32, (1, SEQ), 1) == s
            limit = jnp.sum(jnp.where(at, lens[...], 0), axis=1, keepdims=True)
            scores = jnp.where(position < limit, scores, -jnp.inf)
            top = jnp.max(scores, axis=1, keepdims=True)
            weights = jnp.exp(scores - top)
            probs = (weights / jnp.sum(weights, axis=1, keepdims=True)).astype(BF)
            att_buf[s] = dot_nt(probs, cached[:LAT]).astype(BF)
            return carry

        lax.fori_loop(first_seq, first_seq + n, one, 0)

    def rows_of(chain, du):
        return pl.ds((chain * 4 + du) * 16, 16)

    along = [
        dict(up=plane(0, 1), um=plane(0, 3), vp=plane(1, 0), vm=plane(3, 0)),
        dict(up=plane(1, 0), um=plane(3, 0), vp=plane(0, 1), vm=plane(0, 3)),
    ]
    left_x, right_x = pl.ds(0, QUARTER), pl.ds(QUARTER, WIDE - QUARTER)
    left, right = pl.ds(0, QUARTER), pl.ds(QUARTER, QUARTER)

    u_p, u_m, u_fp, u_fm = [], [], [], []
    v_p, v_m, v_fp, v_fm = [], [], [], []
    for c in range(2):
        d = along[c]
        own = x_ref.at[0, rows_of(c, 0)]
        u_p.append(remote(own, x_ref.at[0, rows_of(c, 3)], d["up"]))
        u_m.append(remote(own, x_ref.at[0, rows_of(c, 1)], d["um"]))
        u_fp.append(
            remote(
                x_ref.at[0, rows_of(c, 3), left_x], x_ref.at[0, rows_of(c, 2), left_x], d["up"]
            )
        )
        u_fm.append(
            remote(
                x_ref.at[0, rows_of(c, 1), right_x], x_ref.at[0, rows_of(c, 2), right_x], d["um"]
            )
        )
        v_p.append([])
        v_m.append([])
        v_fp.append([])
        v_fm.append([])
        for du in range(4):
            r = rows_of(c, du)
            v_p[c].append(remote(x_ref.at[0, r], x_ref.at[3, r], d["vp"]))
            v_m[c].append(remote(x_ref.at[0, r], x_ref.at[1, r], d["vm"]))
            v_fp[c].append(
                remote(x_ref.at[3, r, left_x], x_ref.at[2, r, left_x], d["vp"])
            )
            v_fm[c].append(
                remote(x_ref.at[1, r, right_x], x_ref.at[2, r, right_x], d["vm"])
            )

    for c in range(2):
        for slot in CHAIN_SLOTS[c]:
            z_copies[MIRROR[slot]].wait_recv()
        a, b = CHAIN_SLOTS[c]
        x_ref[0, rows_of(c, 0)] = jnp.concatenate([zbuf[a], zbuf[b]], axis=0)
        u_p[c].start()
        u_m[c].start()
        v_p[c][0].start()
        v_m[c][0].start()

    load_len.wait()
    load_q.wait()
    load_cache.wait()
    attend(0, 2)

    def spread(c, du):
        v_p[c][du].start()
        v_m[c][du].start()

    def forward(c, du):
        v_p[c][du].wait_recv()
        v_fp[c][du].start()
        v_m[c][du].wait_recv()
        v_fm[c][du].start()

    for c in range(2):
        u_p[c].wait_recv()
        u_fp[c].start()
        u_m[c].wait_recv()
        u_fm[c].start()
        spread(c, 3)
        spread(c, 1)

    for copy in piece_copies:
        copy.wait_recv()
    for k in range(8):
        joined = pieces_got[k].astype(F32) + pieces_got[k + 8].astype(F32)
        tx[x, k] = joined.astype(BF)
    before, after = (x + 3) % 4, (x + 1) % 4
    t_p = remote(tx.at[x], tx.at[x], plane(0, 1))
    t_m = remote(tx.at[x], tx.at[x], plane(0, 3))
    t_fp = remote(tx.at[before, pl.ds(0, 4)], tx.at[before, pl.ds(0, 4)], plane(0, 1))
    t_fm = remote(tx.at[after, pl.ds(4, 4)], tx.at[after, pl.ds(4, 4)], plane(0, 3))
    t_p.start()
    t_m.start()

    for c in range(2):
        forward(c, 0)
    for c in range(2):
        u_fp[c].wait_recv()
        u_fm[c].wait_recv()
        spread(c, 2)

    t_p.wait_recv()
    t_fp.start()
    t_m.wait_recv()
    t_fm.start()

    attend(2, 2)

    for c in range(2):
        forward(c, 3)
        forward(c, 1)

    t_fp.wait_recv()
    t_fm.wait_recv()
    for k in range(8):
        block = jnp.concatenate([tx[i, k].astype(F32) for i in range(4)], axis=0)
        t_ref[224 * k : 224 * k + 224] = block.astype(BF)
    for k in range(14):
        block = t_ref[128 * k : 128 * k + 128].astype(F32)
        ct[:, 128 * k : 128 * k + 128] = block.T.astype(BF)
    bq_copy.wait_recv()
    e_copy.wait_recv()
    bpad[...] = jnp.zeros_like(bpad)
    bpad[0:16, 0:HID] = bq_got[0:16]
    bpad[16:32, HID : 2 * HID] = bq_got[16:32]
    epad[...] = jnp.zeros_like(epad)
    for at in (32, 48, 96, 112):
        epad[at : at + 16] = e_got[...]

    load_wg.wait()
    load_wu.wait()
    load_wd.wait()

    lane128 = lax.broadcasted_iota(jnp.int32, (128, 128), 1)
    exchange = [
        remote(gu_own.at[dv], gu_got.at[dv], other_core) for dv in range(4)
    ]

    def first_product(dv):
        gu_own[dv, :, 0:HID] = dot(x_ref[dv, :, 0:HALF], wg[...])
        gu_own[dv, :, HID : 2 * HID] = dot(x_ref[dv, :, 0:HALF], wu[...])
        low_a = dot(x_ref[dv, :, 0:QUARTER], t_ref[...])
        low_b = dot(x_ref[dv, :, QUARTER:HALF], t_ref[...])
        gu_own[dv, :, 2 * HID :] = low_a + pltpu.roll(low_b, 64, 1)
        exchange[dv].start()

    def second_product(dv):
        exchange[dv].wait_recv()
        low = (gu_own[dv, :, 2 * HID :] + gu_got[dv, :, 2 * HID :]).astype(BF)
        extra = dot(low, bpad[...])
        gate = gu_own[dv, :, 0:HID] + gu_got[dv, :, 0:HID] + extra[:, 0:HID]
        up = gu_own[dv, :, HID : 2 * HID] + gu_got[dv, :, HID : 2 * HID] + extra[:, HID:]
        hidden = (gate / (1.0 + jnp.exp(-gate)) * up).astype(BF)
        narrow = dot_nt(hidden, epad[...])
        head = narrow.astype(BF).astype(F32)
        rest = narrow - head
        split = jnp.where((lane128 % 64) < 48, head, rest)
        picks = (lane128 % 32 == expert) & (lane128 < 96)
        shares = x_ref[dv, :, HALF:WIDE].astype(F32)
        share = jnp.sum(jnp.where(picks, shares, 0.0), axis=1, keepdims=True)
        for h in range(2):
            keep = (lane128 // 64) == h
            thin = jnp.where(keep, split, 0.0).astype(BF)

            def tile(i, carry):
                at = pl.multiple_of(i * HID, HID)
                there = pl.multiple_of(h * QUARTER + i * HID, HID)
                value = dot(hidden, wd[:, pl.ds(there, HID)]) + dot(thin, ct[:, pl.ds(at, HID)])
                p_ref[dv, :, pl.ds(there, HID)] = (value * share).astype(BF)
                return carry

            lax.fori_loop(0, QUARTER // HID, tile, 0)

    first_product(0)
    for c in range(2):
        forward(c, 2)
    first_product(1)
    first_product(3)
    second_product(0)

    a_p, a_m, b_p, b_m, c_p, c_m = [], [], [], [], [], []
    for c in range(2):
        d = along[c]
        for group in (a_p, a_m, b_p, b_m, c_p, c_m):
            group.append([])
        for du in range(4):
            r = rows_of(c, du)
            a_p[c].append(remote(p_ref.at[2, r, left], ra.at[0, r], d["vp"]))
            a_m[c].append(remote(p_ref.at[2, r, right], ra.at[1, r], d["vm"]))
            b_p[c].append(remote(p_ref.at[1, r, right], from_left.at[r, right], d["vp"]))
            b_m[c].append(remote(p_ref.at[3, r, left], from_right.at[r, left], d["vm"]))
            c_p[c].append(remote(p_ref.at[1, r, left], from_left.at[r, left], d["vp"]))
            c_m[c].append(remote(p_ref.at[3, r, right], from_right.at[r, right], d["vm"]))
    order = (2, 1, 3, 0)

    second_product(1)
    for c in range(2):
        for du in order:
            b_p[c][du].start()
    second_product(3)
    for c in range(2):
        for du in order:
            b_m[c][du].start()
    for c in range(2):
        for du in range(4):
            v_fp[c][du].wait_recv()
            v_fm[c][du].wait_recv()
    first_product(2)
    attend(4, 1)
    second_product(2)
    for du in order:
        for c in range(2):
            a_p[c][du].start()
            a_m[c][du].start()
    attend(5, 3)
    store_att = local(att_buf, att_hbm.at[0])

    for copy in z_copies + [bq_copy, e_copy] + piece_copies + [t_p, t_m, t_fp, t_fm]:
        copy.wait_send()
    for c in range(2):
        for copy in [u_p[c], u_m[c], u_fp[c], u_fm[c]] + v_p[c] + v_m[c] + v_fp[c] + v_fm[c]:
            copy.wait_send()
    for copy in exchange:
        copy.wait_send()

    for du in order:
        for c in range(2):
            r = rows_of(c, du)
            a_p[c][du].wait_recv()
            p_ref[1, r, left] = (p_ref[1, r, left].astype(F32) + ra[0, r].astype(F32)).astype(BF)
            c_p[c][du].start()
            a_m[c][du].wait_recv()
            p_ref[3, r, right] = (p_ref[3, r, right].astype(F32) + ra[1, r].astype(F32)).astype(BF)
            c_m[c][du].start()

    def gather_v(c, du):
        r = rows_of(c, du)
        for copy in (b_p[c][du], c_p[c][du], b_m[c][du], c_m[c][du]):
            copy.wait_recv()
        total = p_ref[0, r].astype(F32) + from_left[r].astype(F32) + from_right[r].astype(F32)
        q_sum[r] = total.astype(BF)

    a2p, a2m, b2p, b2m, c2p, c2m = [], [], [], [], [], []
    for c in range(2):
        d = along[c]
        r1, r2, r3 = rows_of(c, 1), rows_of(c, 2), rows_of(c, 3)
        a2p.append(remote(q_sum.at[r2, left], ra2.at[0, c], d["up"]))
        a2m.append(remote(q_sum.at[r2, right], ra2.at[1, c], d["um"]))
        b2p.append(remote(q_sum.at[r1, right], from_left2.at[c, :, right], d["up"]))
        b2m.append(remote(q_sum.at[r3, left], from_right2.at[c, :, left], d["um"]))
        c2p.append(remote(q_sum.at[r1, left], from_left2.at[c, :, left], d["up"]))
        c2m.append(remote(q_sum.at[r3, right], from_right2.at[c, :, right], d["um"]))
    for c in range(2):
        gather_v(c, 2)
        a2p[c].start()
        a2m[c].start()
    for c in range(2):
        gather_v(c, 1)
        b2p[c].start()
    for c in range(2):
        gather_v(c, 3)
        b2m[c].start()
    for c in range(2):
        r1, r3 = rows_of(c, 1), rows_of(c, 3)
        a2p[c].wait_recv()
        q_sum[r1, left] = (q_sum[r1, left].astype(F32) + ra2[0, c].astype(F32)).astype(BF)
        c2p[c].start()
        a2m[c].wait_recv()
        q_sum[r3, right] = (q_sum[r3, right].astype(F32) + ra2[1, c].astype(F32)).astype(BF)
        c2m[c].start()
    for c in range(2):
        gather_v(c, 0)

    z_back = [remote(z_send.at[slot], z_got.at[MIRROR[slot]], across(STEPS[slot], 0)) for slot in range(4)]
    for c in range(2):
        for copy in (b2p[c], c2p[c], b2m[c], c2m[c]):
            copy.wait_recv()
        total = (
            q_sum[rows_of(c, 0)].astype(F32)
            + from_left2[c].astype(F32)
            + from_right2[c].astype(F32)
        )
        for i in range(2):
            slot = CHAIN_SLOTS[c][i]
            z_send[slot] = total[8 * i : 8 * i + 8].astype(BF)
            z_back[slot].start()

    for c in range(2):
        for group in (a_p, a_m, b_p, b_m, c_p, c_m):
            for copy in group[c]:
                copy.wait_send()
        for copy in (a2p[c], a2m[c], b2p[c], b2m[c], c2p[c], c2m[c]):
            copy.wait_send()
    store_att.wait()
    for copy in z_back:
        copy.wait_recv()
    result = z_got[0].astype(F32) + z_got[1].astype(F32) + z_got[2].astype(F32) + z_got[3].astype(F32)
    out_buf[...] = result.astype(BF)
    store_out = local(out_buf, expert_hbm.at[0])
    for copy in z_back:
        copy.wait_send()
    store_out.wait()
    assert count[0] == N_COPIES, count[0]


def body(
    queries,
    latent_rotary_cache,
    lengths,
    section_hidden_rows,
    row_expert_index,
    routing_gate_weight,
    gate_matrix,
    up_weight,
    down_weight,
    adapter_input_factor,
    adapter_output_factor,
    adapter_up_output,
    adapter_down_input,
):
    vmem = pltpu.VMEM
    expert_out, attention_out = pl.pallas_call(
        kernel,
        out_shape=(
            jax.ShapeDtypeStruct((1, SEQ, HALF), BF),
            jax.ShapeDtypeStruct((1, SEQ, HEADS, LAT), BF),
        ),
        in_specs=[pl.BlockSpec(memory_space=pl.ANY)] * 13,
        out_specs=[pl.BlockSpec(memory_space=pl.ANY)] * 2,
        scratch_shapes=[
            vmem((SEQ, WIDE), BF),
            vmem((4, SEQ, WIDE), BF),
            vmem((4, 128, WIDE), BF),
            vmem((4, 128, 2 * HID + 128), F32),
            vmem((4, 128, 2 * HID + 128), F32),
            vmem((4, 128, HALF), BF),
            vmem((2, 128, QUARTER), BF),
            vmem((128, HALF), BF),
            vmem((128, HALF), BF),
            vmem((128, HALF), BF),
            vmem((2, 2, 16, QUARTER), BF),
            vmem((2, 16, HALF), BF),
            vmem((2, 16, HALF), BF),
            vmem((4, SEQ, HALF), BF),
            vmem((4, SEQ, HALF), BF),
            vmem((SEQ, HALF), BF),
            vmem((HALF, HID), BF),
            vmem((HALF, HID), BF),
            vmem((HID, HALF), BF),
            vmem((SLICE, 512), BF),
            vmem((SLICE, 256), BF),
            vmem((32, HID), BF),
            vmem((16, HID), BF),
            vmem((16, SLICE, 128), BF),
            vmem((16, SLICE, 128), BF),
            vmem((4, 8, SLICE, 128), BF),
            vmem((QUARTER, 128), BF),
            vmem((128, QUARTER), BF),
            vmem((128, 2 * HID), BF),
            vmem((128, HID), BF),
            vmem((SEQ, HEADS, KD), BF),
            vmem((SEQ, KD, LEN), BF),
            vmem((1, SEQ), jnp.int32),
            vmem((SEQ, 8), jnp.int32),
            vmem((SEQ, 8), F32),
            vmem((SEQ, HEADS, LAT), BF),
            pltpu.SemaphoreType.DMA((N_COPIES,)),
            pltpu.SemaphoreType.DMA((N_COPIES,)),
            pltpu.SemaphoreType.DMA((N_LOCAL,)),
        ],
        compiler_params=pltpu.CompilerParams(
            collective_id=0, has_side_effects=True, vmem_limit_bytes=56 * 1024 * 1024
        ),
    )(
        queries,
        jnp.swapaxes(latent_rotary_cache, 2, 3),
        lengths,
        section_hidden_rows,
        row_expert_index,
        routing_gate_weight,
        gate_matrix,
        up_weight,
        down_weight,
        adapter_input_factor,
        adapter_output_factor,
        adapter_up_output,
        adapter_down_input,
    )
    return (expert_out, attention_out)


def solution(mesh):
    return jax.shard_map(
        body,
        mesh=mesh,
        in_specs=(
            P("sect", "grp", "tp", None),
            P("sect", "grp", None, None),
            P("sect", "grp"),
            P("sect", "grp", "tp"),
            P("sect", "grp", None),
            P("sect", "grp", None),
            P("sect", "tp", "grp"),
            P("sect", "tp", "grp"),
            P("sect", "grp", "tp"),
            P("sect", "tp", "grp", None),
            P("sect", "tp", "grp", None),
            P("sect", None, "grp"),
            P("sect", None, "grp"),
        ),
        out_specs=(P("sect", "grp", "tp"), P("sect", "grp", "tp", None)),
        check_vma=False,
    )
```

```python
import jax
import jax.numpy as jnp
from jax import lax
from jax.experimental import pallas as pl
from jax.experimental.pallas import tpu as pltpu
from jax.sharding import PartitionSpec as P

LAT = 512
QK = 192
SEQ = 8
HEADS = 64
KD = 576
LEN = 512
HALF = 3584
QUARTER = HALF // 2
WIDE = HALF + 128
HID = 256
SLICE = 56
N_COPIES = 133
N_LOCAL = 16
BF = jnp.bfloat16
F32 = jnp.float32
MESH = pl.DeviceIdType.MESH

STEPS = (1, -1, 3, -3)
MIRROR = (1, 0, 3, 2)
CHAIN_SLOTS = ((0, 1), (2, 3))


def dot(a, b):
    return jnp.dot(a, b, preferred_element_type=F32)


def dot_nt(a, b):
    return lax.dot_general(a, b, (((1,), (1,)), ((), ())), preferred_element_type=F32)


def kernel(
    q_hbm,
    cache_hbm,
    len_hbm,
    rows_hbm,
    ids_hbm,
    gates_hbm,
    wg_hbm,
    wu_hbm,
    wd_hbm,
    ain_hbm,
    cout_hbm,
    bq_hbm,
    e_hbm,
    z_got,
    att_hbm,
    unit,
    zbuf,
    x_ref,
    gu_own,
    gu_got,
    p_ref,
    ra,
    from_left,
    from_right,
    q_sum,
    ra2,
    from_left2,
    from_right2,
    z_send,
    wg,
    wu,
    wd,
    ain,
    cout,
    bq_got,
    e_got,
    pieces,
    pieces_got,
    joined,
    tx,
    t_ref,
    ct,
    bpad,
    epad,
    q_buf,
    cache,
    lens,
    ids,
    gates,
    att_buf,
    send_sem,
    recv_sem,
    local_sem,
):
    sect = lax.axis_index("sect")
    grp = lax.axis_index("grp")
    tp = lax.axis_index("tp")
    y = grp // 16
    zh = (grp // 4) % 4
    x = grp % 4
    z = zh * 2 + sect
    expert = grp // 4

    def plane(dy, dx):
        return (sect, ((y + dy) % 4) * 16 + zh * 4 + (x + dx) % 4, tp)

    def across(step):
        target = (z + step + 8) % 8
        return (target % 2, y * 16 + (target // 2) * 4 + x, tp)

    other_core = (sect, grp, 1 - tp)
    partner = (1 - sect, grp, tp)
    count = [0]

    def remote(src, dst, device):
        i = count[0]
        count[0] += 1
        return pltpu.make_async_remote_copy(
            src_ref=src,
            dst_ref=dst,
            send_sem=send_sem.at[i],
            recv_sem=recv_sem.at[i],
            device_id=device,
            device_id_type=MESH,
        )

    local_count = [0]

    def local(src, dst):
        i = local_count[0]
        local_count[0] += 1
        copy = pltpu.make_async_copy(src, dst, local_sem.at[i])
        copy.start()
        return copy

    barrier = pltpu.get_barrier_semaphore()
    peers = [other_core, plane(1, 0), plane(2, 0), plane(3, 0), plane(0, 1), plane(0, 3)]
    peers += [across(step) for step in STEPS]
    for peer in peers:
        pl.semaphore_signal(barrier, inc=1, device_id=peer, device_id_type=MESH)

    load_rows = local(rows_hbm.at[0], unit.at[:, pl.ds(0, HALF)])
    load_ids = local(ids_hbm.at[0], ids)
    load_gates = local(gates_hbm.at[0], gates)
    load_ain = local(ain_hbm.at[0, 0], ain)
    load_cout = local(cout_hbm.at[0, 0], cout)
    load_len = local(len_hbm, lens)
    load_q = local(q_hbm.at[0], q_buf)
    load_cache = local(cache_hbm.at[0], cache)
    load_wg = local(wg_hbm.at[0], wg)
    load_wu = local(wu_hbm.at[0], wu)
    load_wd = local(wd_hbm.at[0], wd)

    load_ids.wait()
    load_gates.wait()
    lane8 = lax.broadcasted_iota(jnp.int32, (SEQ, 128), 1)
    named = lane8 % 32
    share = jnp.zeros((SEQ, 128), F32)
    for k in range(8):
        share += jnp.where(ids[:, k : k + 1] == named, gates[:, k : k + 1], 0.0)
    first = share.astype(BF).astype(F32)
    second = (share - first).astype(BF).astype(F32)
    third = share - first - second
    terms = jnp.where(lane8 < 32, first, jnp.where(lane8 < 64, second, third))
    load_rows.wait()
    unit[:, HALF:WIDE] = jnp.where(lane8 < 96, terms, 0.0).astype(BF)

    pl.semaphore_wait(barrier, len(peers))

    z_copies = [
        remote(unit, zbuf.at[MIRROR[slot]], across(STEPS[slot])) for slot in range(4)
    ]
    for copy in z_copies:
        copy.start()
    bq_copy = remote(bq_hbm.at[0], bq_got, partner)
    e_copy = remote(e_hbm.at[0], e_got, partner)
    bq_copy.start()
    e_copy.start()

    load_ain.wait()
    load_cout.wait()
    lane56 = lax.broadcasted_iota(jnp.int32, (SLICE, 128), 1)
    shift = (y // 2) * 64
    mine = (lane56 >= shift) & (lane56 < shift + 64)
    place = lane56 % 64
    for e in range(16):
        a_tile = ain[:, 128 * (e // 4) : 128 * (e // 4) + 128].astype(F32)
        c_tile = cout[:, 128 * (e // 8) : 128 * (e // 8) + 128].astype(F32)
        a_at, c_at = 32 * (e % 4), 16 * (e % 8)

        def turned(tile, by):
            by = by % 128
            return tile if by == 0 else pltpu.roll(tile, by, 1)

        low = jnp.where(
            place < 32,
            turned(a_tile, -a_at),
            jnp.where(place < 48, turned(c_tile, 32 - c_at), turned(c_tile, 48 - c_at)),
        )
        low = jnp.where(lane56 < 64, low, 0.0)
        both = low + pltpu.roll(low, 64, 1)
        pieces[e] = jnp.where(mine, both, 0.0).astype(BF)
    y_copies = [
        remote(
            pieces.at[pl.ds(((y + dy) % 4) * 4, 4)], pieces_got.at[y], plane(dy, 0)
        )
        for dy in (1, 3, 2)
    ]
    for copy in y_copies:
        copy.start()
    pieces_got[y] = pieces[pl.ds(y * 4, 4)]

    def attend(first_seq, n):
        def one(s, carry):
            cached = cache[s]
            query = q_buf[s]
            scores = dot(query[:, :LAT], cached[:LAT]) + dot(query[:, LAT:], cached[LAT:])
            scores = scores * QK ** (-0.5)
            position = lax.broadcasted_iota(jnp.int32, (HEADS, LEN), 1)
            at = lax.broadcasted_iota(jnp.int32, (1, SEQ), 1) == s
            limit = jnp.sum(jnp.where(at, lens[...], 0), axis=1, keepdims=True)
            scores = jnp.where(position < limit, scores, -jnp.inf)
            top = jnp.max(scores, axis=1, keepdims=True)
            weights = jnp.exp(scores - top)
            probs = (weights / jnp.sum(weights, axis=1, keepdims=True)).astype(BF)
            att_buf[s] = dot_nt(probs, cached[:LAT]).astype(BF)
            return carry

        lax.fori_loop(first_seq, first_seq + n, one, 0)

    def rows_of(chain, du):
        return pl.ds((chain * 4 + du) * 16, 16)

    along = [
        dict(up=plane(0, 1), um=plane(0, 3), vp=plane(1, 0), vm=plane(3, 0)),
        dict(up=plane(1, 0), um=plane(3, 0), vp=plane(0, 1), vm=plane(0, 3)),
    ]
    left_x, right_x = pl.ds(0, QUARTER), pl.ds(QUARTER, WIDE - QUARTER)
    left, right = pl.ds(0, QUARTER), pl.ds(QUARTER, QUARTER)

    u_p, u_m, u_fp, u_fm = [], [], [], []
    v_p, v_m, v_fp, v_fm = [], [], [], []
    for c in range(2):
        d = along[c]
        own = x_ref.at[0, rows_of(c, 0)]
        u_p.append(remote(own, x_ref.at[0, rows_of(c, 3)], d["up"]))
        u_m.append(remote(own, x_ref.at[0, rows_of(c, 1)], d["um"]))
        u_fp.append(
            remote(
                x_ref.at[0, rows_of(c, 3), left_x], x_ref.at[0, rows_of(c, 2), left_x], d["up"]
            )
        )
        u_fm.append(
            remote(
                x_ref.at[0, rows_of(c, 1), right_x], x_ref.at[0, rows_of(c, 2), right_x], d["um"]
            )
        )
        v_p.append([])
        v_m.append([])
        v_fp.append([])
        v_fm.append([])
        for du in range(4):
            r = rows_of(c, du)
            v_p[c].append(remote(x_ref.at[0, r], x_ref.at[3, r], d["vp"]))
            v_m[c].append(remote(x_ref.at[0, r], x_ref.at[1, r], d["vm"]))
            v_fp[c].append(
                remote(x_ref.at[3, r, left_x], x_ref.at[2, r, left_x], d["vp"])
            )
            v_fm[c].append(
                remote(x_ref.at[1, r, right_x], x_ref.at[2, r, right_x], d["vm"])
            )

    def enter(c):
        for slot in CHAIN_SLOTS[c]:
            z_copies[MIRROR[slot]].wait_recv()
        a, b = CHAIN_SLOTS[c]
        x_ref[0, rows_of(c, 0)] = jnp.concatenate([zbuf[a], zbuf[b]], axis=0)
        u_p[c].start()
        u_m[c].start()
        v_p[c][0].start()
        v_m[c][0].start()

    def spread(c, du):
        v_p[c][du].start()
        v_m[c][du].start()

    def forward(c, du):
        v_p[c][du].wait_recv()
        v_fp[c][du].start()
        v_m[c][du].wait_recv()
        v_fm[c][du].start()

    def turn(c):
        u_p[c].wait_recv()
        u_fp[c].start()
        u_m[c].wait_recv()
        u_fm[c].start()
        spread(c, 3)
        spread(c, 1)

    def turn_far(c):
        u_fp[c].wait_recv()
        u_fm[c].wait_recv()
        spread(c, 2)

    enter(0)

    for copy in y_copies:
        copy.wait_recv()
    for k in range(4):
        for i in range(2):
            both = pieces_got[i, k].astype(F32) + pieces_got[i + 2, k].astype(F32)
            joined[k, i] = both.astype(BF)
    t_copies = [
        remote(joined.at[((z + step + 8) % 8) // 2], tx.at[x, zh], across(step)) for step in STEPS
    ]
    for copy in t_copies:
        copy.start()

    enter(1)
    load_len.wait()
    load_q.wait()
    load_cache.wait()
    attend(0, 1)
    turn(0)
    attend(1, 1)
    turn(1)

    for copy in t_copies:
        copy.wait_recv()
    before, after = (x + 3) % 4, (x + 1) % 4
    t_p = remote(tx.at[x], tx.at[x], plane(0, 1))
    t_m = remote(tx.at[x], tx.at[x], plane(0, 3))
    t_fp = remote(tx.at[before, pl.ds(0, 2)], tx.at[before, pl.ds(0, 2)], plane(0, 1))
    t_fm = remote(tx.at[after, pl.ds(2, 2)], tx.at[after, pl.ds(2, 2)], plane(0, 3))
    t_p.start()
    t_m.start()

    forward(0, 0)
    turn_far(0)
    forward(1, 0)
    turn_far(1)

    bq_copy.wait_recv()
    e_copy.wait_recv()
    bpad[...] = jnp.zeros_like(bpad)
    bpad[0:16, 0:HID] = bq_got[0:16]
    bpad[16:32, HID : 2 * HID] = bq_got[16:32]
    epad[...] = jnp.zeros_like(epad)
    for at in (32, 48, 96, 112):
        epad[at : at + 16] = e_got[...]

    lane128 = lax.broadcasted_iota(jnp.int32, (128, 128), 1)
    low_at, gate_at, up_at = (
        pl.ds(2 * HID, 128),
        pl.ds(0, HID),
        pl.ds(HID, HID),
    )
    exchange = [
        [
            remote(gu_own.at[dv, :, at], gu_got.at[dv, :, at], other_core)
            for at in (gate_at, up_at, low_at)
        ]
        for dv in range(4)
    ]

    def wide_product(dv):
        gu_own[dv, :, gate_at] = dot(x_ref[dv, :, 0:HALF], wg[...])
        exchange[dv][0].start()
        gu_own[dv, :, up_at] = dot(x_ref[dv, :, 0:HALF], wu[...])
        exchange[dv][1].start()

    def low_product(dv):
        low_a = dot(x_ref[dv, :, 0:QUARTER], t_ref[...])
        low_b = dot(x_ref[dv, :, QUARTER:HALF], t_ref[...])
        gu_own[dv, :, low_at] = low_a + pltpu.roll(low_b, 64, 1)
        exchange[dv][2].start()

    def second_product(dv, after=None):
        exchange[dv][2].wait_recv()
        low = (gu_own[dv, :, low_at] + gu_got[dv, :, low_at]).astype(BF)
        extra = dot(low, bpad[...])
        exchange[dv][0].wait_recv()
        gate = gu_own[dv, :, gate_at] + gu_got[dv, :, gate_at] + extra[:, 0:HID]
        silu = gate / (1.0 + jnp.exp(-gate))
        exchange[dv][1].wait_recv()
        up = gu_own[dv, :, up_at] + gu_got[dv, :, up_at] + extra[:, HID:]
        hidden = (silu * up).astype(BF)
        narrow = dot_nt(hidden, epad[...])
        head = narrow.astype(BF).astype(F32)
        rest = narrow - head
        split = jnp.where((lane128 % 64) < 48, head, rest)
        picks = (lane128 % 32 == expert) & (lane128 < 96)
        shares = x_ref[dv, :, HALF:WIDE].astype(F32)
        share = jnp.sum(jnp.where(picks, shares, 0.0), axis=1, keepdims=True)
        for h in range(2):
            thin = jnp.where((lane128 // 64) == h, split, 0.0).astype(BF)
            for i in range(QUARTER // HID):
                at = i * HID
                there = h * QUARTER + at
                value = dot(hidden, wd[:, there : there + HID]) + dot(thin, ct[:, at : at + HID])
                p_ref[dv, :, there : there + HID] = (value * share).astype(BF)
            if after is not None:
                after(h)

    load_wg.wait()
    load_wu.wait()
    wide_product(0)

    t_p.wait_recv()
    t_fp.start()
    t_m.wait_recv()
    t_fm.start()
    attend(2, 2)

    for c in range(2):
        forward(c, 3)
    for c in range(2):
        forward(c, 1)

    t_fp.wait_recv()
    t_fm.wait_recv()
    for i in range(2):
        for k in range(4):
            block = jnp.concatenate([tx[j, k, i].astype(F32) for j in range(4)], axis=0)
            t_ref[224 * (4 * i + k) : 224 * (4 * i + k) + 224] = block.astype(BF)
    for k in range(14):
        block = t_ref[128 * k : 128 * k + 128].astype(F32)
        ct[:, 128 * k : 128 * k + 128] = block.T.astype(BF)
    low_product(0)
    load_wd.wait()
    attend(4, 1)
    second_product(0)

    for c in range(2):
        forward(c, 2)
    low_product(1)
    wide_product(1)
    low_product(3)
    wide_product(3)

    a_p, a_m, b_p, b_m, c_p, c_m = [], [], [], [], [], []
    for c in range(2):
        d = along[c]
        for group in (a_p, a_m, b_p, b_m, c_p, c_m):
            group.append([])
        for du in range(4):
            r = rows_of(c, du)
            a_p[c].append(remote(p_ref.at[2, r, left], ra.at[0, r], d["vp"]))
            a_m[c].append(remote(p_ref.at[2, r, right], ra.at[1, r], d["vm"]))
            b_p[c].append(remote(p_ref.at[1, r, right], from_left.at[r, right], d["vp"]))
            b_m[c].append(remote(p_ref.at[3, r, left], from_right.at[r, left], d["vm"]))
            c_p[c].append(remote(p_ref.at[1, r, left], from_left.at[r, left], d["vp"]))
            c_m[c].append(remote(p_ref.at[3, r, right], from_right.at[r, right], d["vm"]))
    order = (2, 1, 3, 0)

    second_product(1)
    for du in order:
        for c in range(2):
            b_p[c][du].start()
    second_product(3)
    for du in order:
        for c in range(2):
            b_m[c][du].start()
    for c in range(2):
        for du in range(4):
            v_fp[c][du].wait_recv()
            v_fm[c][du].wait_recv()
    low_product(2)
    wide_product(2)

    def begin_return(h):
        for du in order:
            for c in range(2):
                (a_p, a_m)[h][c][du].start()

    second_product(2, begin_return)
    attend(5, 3)
    store_att = local(att_buf, att_hbm.at[0])

    def carry_v(du):
        for c in range(2):
            r = rows_of(c, du)
            a_p[c][du].wait_recv()
            p_ref[1, r, left] = (p_ref[1, r, left].astype(F32) + ra[0, r].astype(F32)).astype(BF)
            c_p[c][du].start()
            a_m[c][du].wait_recv()
            p_ref[3, r, right] = (p_ref[3, r, right].astype(F32) + ra[1, r].astype(F32)).astype(BF)
            c_m[c][du].start()

    def gather_v(c, du):
        r = rows_of(c, du)
        for copy in (b_p[c][du], c_p[c][du], b_m[c][du], c_m[c][du]):
            copy.wait_recv()
        total = p_ref[0, r].astype(F32) + from_left[r].astype(F32) + from_right[r].astype(F32)
        q_sum[r] = total.astype(BF)

    a2p, a2m, b2p, b2m, c2p, c2m = [], [], [], [], [], []
    for c in range(2):
        d = along[c]
        r1, r2, r3 = rows_of(c, 1), rows_of(c, 2), rows_of(c, 3)
        a2p.append(remote(q_sum.at[r2, left], ra2.at[0, c], d["up"]))
        a2m.append(remote(q_sum.at[r2, right], ra2.at[1, c], d["um"]))
        b2p.append(remote(q_sum.at[r1, right], from_left2.at[c, :, right], d["up"]))
        b2m.append(remote(q_sum.at[r3, left], from_right2.at[c, :, left], d["um"]))
        c2p.append(remote(q_sum.at[r1, left], from_left2.at[c, :, left], d["up"]))
        c2m.append(remote(q_sum.at[r3, right], from_right2.at[c, :, right], d["um"]))
    carry_v(2)
    carry_v(1)
    for c in range(2):
        gather_v(c, 2)
        a2p[c].start()
        a2m[c].start()
    carry_v(3)
    for c in range(2):
        gather_v(c, 1)
        b2p[c].start()
    carry_v(0)
    for c in range(2):
        gather_v(c, 3)
        b2m[c].start()

    for copy in z_copies + [bq_copy, e_copy] + y_copies + t_copies + [t_p, t_m, t_fp, t_fm]:
        copy.wait_send()
    for c in range(2):
        for copy in [u_p[c], u_m[c], u_fp[c], u_fm[c]] + v_p[c] + v_m[c] + v_fp[c] + v_fm[c]:
            copy.wait_send()
    for dv in range(4):
        for copy in exchange[dv]:
            copy.wait_send()

    for c in range(2):
        r1, r3 = rows_of(c, 1), rows_of(c, 3)
        a2p[c].wait_recv()
        q_sum[r1, left] = (q_sum[r1, left].astype(F32) + ra2[0, c].astype(F32)).astype(BF)
        c2p[c].start()
        a2m[c].wait_recv()
        q_sum[r3, right] = (q_sum[r3, right].astype(F32) + ra2[1, c].astype(F32)).astype(BF)
        c2m[c].start()
    for c in range(2):
        gather_v(c, 0)

    z_back = [remote(z_send.at[slot], z_got.at[MIRROR[slot]], across(STEPS[slot])) for slot in range(4)]
    for c in range(2):
        for copy in (b2p[c], c2p[c], b2m[c], c2m[c]):
            copy.wait_recv()
        total = (
            q_sum[rows_of(c, 0)].astype(F32)
            + from_left2[c].astype(F32)
            + from_right2[c].astype(F32)
        )
        for i in range(2):
            slot = CHAIN_SLOTS[c][i]
            z_send[slot] = total[8 * i : 8 * i + 8].astype(BF)
            z_back[slot].start()

    for c in range(2):
        for group in (a_p, a_m, b_p, b_m, c_p, c_m):
            for copy in group[c]:
                copy.wait_send()
        for copy in (a2p[c], a2m[c], b2p[c], b2m[c], c2p[c], c2m[c]):
            copy.wait_send()
    store_att.wait()
    for copy in z_back:
        copy.wait_recv()
    for copy in z_back:
        copy.wait_send()
    assert count[0] == N_COPIES, count[0]


def finish(z_got, att_in, expert_hbm, att_hbm, parts, out_buf, att_buf, sems):
    load = pltpu.make_async_copy(z_got, parts, sems.at[0])
    load.start()
    load_att = pltpu.make_async_copy(att_in, att_buf, sems.at[1])
    load_att.start()
    load.wait()
    total = parts[0].astype(F32) + parts[1].astype(F32) + parts[2].astype(F32) + parts[3].astype(F32)
    out_buf[...] = total.astype(BF)
    store = pltpu.make_async_copy(out_buf, expert_hbm.at[0], sems.at[2])
    store.start()
    load_att.wait()
    store_att = pltpu.make_async_copy(att_buf, att_hbm, sems.at[3])
    store_att.start()
    store.wait()
    store_att.wait()


def body(
    queries,
    latent_rotary_cache,
    lengths,
    section_hidden_rows,
    row_expert_index,
    routing_gate_weight,
    gate_matrix,
    up_weight,
    down_weight,
    adapter_input_factor,
    adapter_output_factor,
    adapter_up_output,
    adapter_down_input,
):
    vmem = pltpu.VMEM
    returned, attended = pl.pallas_call(
        kernel,
        out_shape=(
            jax.ShapeDtypeStruct((4, SEQ, HALF), BF),
            jax.ShapeDtypeStruct((1, SEQ, HEADS, LAT), BF),
        ),
        in_specs=[pl.BlockSpec(memory_space=pl.ANY)] * 13,
        out_specs=[pl.BlockSpec(memory_space=pl.ANY)] * 2,
        scratch_shapes=[
            vmem((SEQ, WIDE), BF),
            vmem((4, SEQ, WIDE), BF),
            vmem((4, 128, WIDE), BF),
            vmem((4, 128, 2 * HID + 128), F32),
            vmem((4, 128, 2 * HID + 128), F32),
            vmem((4, 128, HALF), BF),
            vmem((2, 128, QUARTER), BF),
            vmem((128, HALF), BF),
            vmem((128, HALF), BF),
            vmem((128, HALF), BF),
            vmem((2, 2, 16, QUARTER), BF),
            vmem((2, 16, HALF), BF),
            vmem((2, 16, HALF), BF),
            vmem((4, SEQ, HALF), BF),
            vmem((HALF, HID), BF),
            vmem((HALF, HID), BF),
            vmem((HID, HALF), BF),
            vmem((SLICE, 512), BF),
            vmem((SLICE, 256), BF),
            vmem((32, HID), BF),
            vmem((16, HID), BF),
            vmem((16, SLICE, 128), BF),
            vmem((4, 4, SLICE, 128), BF),
            vmem((4, 2, SLICE, 128), BF),
            vmem((4, 4, 2, SLICE, 128), BF),
            vmem((QUARTER, 128), BF),
            vmem((128, QUARTER), BF),
            vmem((128, 2 * HID), BF),
            vmem((128, HID), BF),
            vmem((SEQ, HEADS, KD), BF),
            vmem((SEQ, KD, LEN), BF),
            vmem((1, SEQ), jnp.int32),
            vmem((SEQ, 8), jnp.int32),
            vmem((SEQ, 8), F32),
            vmem((SEQ, HEADS, LAT), BF),
            pltpu.SemaphoreType.DMA((N_COPIES,)),
            pltpu.SemaphoreType.DMA((N_COPIES,)),
            pltpu.SemaphoreType.DMA((N_LOCAL,)),
        ],
        compiler_params=pltpu.CompilerParams(
            collective_id=0, has_side_effects=True, vmem_limit_bytes=56 * 1024 * 1024
        ),
    )(
        queries,
        jnp.swapaxes(latent_rotary_cache, 2, 3),
        lengths,
        section_hidden_rows,
        row_expert_index,
        routing_gate_weight,
        gate_matrix,
        up_weight,
        down_weight,
        adapter_input_factor,
        adapter_output_factor,
        adapter_up_output,
        adapter_down_input,
    )
    return pl.pallas_call(
        finish,
        out_shape=(
            jax.ShapeDtypeStruct((1, SEQ, HALF), BF),
            jax.ShapeDtypeStruct((1, SEQ, HEADS, LAT), BF),
        ),
        in_specs=[pl.BlockSpec(memory_space=pltpu.HBM)] * 2,
        out_specs=[pl.BlockSpec(memory_space=pltpu.HBM)] * 2,
        scratch_shapes=[
            vmem((4, SEQ, HALF), BF),
            vmem((SEQ, HALF), BF),
            vmem((1, SEQ, HEADS, LAT), BF),
            pltpu.SemaphoreType.DMA((4,)),
        ],
    )(returned, attended)


def solution(mesh):
    return jax.shard_map(
        body,
        mesh=mesh,
        in_specs=(
            P("sect", "grp", "tp", None),
            P("sect", "grp", None, None),
            P("sect", "grp"),
            P("sect", "grp", "tp"),
            P("sect", "grp", None),
            P("sect", "grp", None),
            P("sect", "tp", "grp"),
            P("sect", "tp", "grp"),
            P("sect", "grp", "tp"),
            P("sect", "tp", "grp", None),
            P("sect", "tp", "grp", None),
            P("sect", None, "grp"),
            P("sect", None, "grp"),
        ),
        out_specs=(P("sect", "grp", "tp"), P("sect", "grp", "tp", None)),
        check_vma=False,
    )
```

```python
import jax
import jax.numpy as jnp
from jax import lax
from jax.experimental import pallas as pl
from jax.experimental.pallas import tpu as pltpu
from jax.sharding import PartitionSpec as P

LAT = 512
QK = 192
SEQ = 8
HEADS = 64
KD = 576
LEN = 512
HALF = 3584
QUARTER = HALF // 2
WIDE = HALF + 128
HID = 256
SLICE = 56
N_COPIES = 133
N_LOCAL = 16
BF = jnp.bfloat16
F32 = jnp.float32
MESH = pl.DeviceIdType.MESH

STEPS = (1, -1, 3, -3)
MIRROR = (1, 0, 3, 2)
CHAIN_SLOTS = ((0, 1), (2, 3))


def dot(a, b):
    return jnp.dot(a, b, preferred_element_type=F32)


def dot_nt(a, b):
    return lax.dot_general(a, b, (((1,), (1,)), ((), ())), preferred_element_type=F32)


def kernel(
    q_hbm,
    cache_hbm,
    len_hbm,
    rows_hbm,
    ids_hbm,
    gates_hbm,
    wg_hbm,
    wu_hbm,
    wd_hbm,
    ain_hbm,
    cout_hbm,
    bq_hbm,
    e_hbm,
    z_got,
    att_hbm,
    unit,
    zbuf,
    x_ref,
    gu_own,
    gu_got,
    p_ref,
    ra,
    from_left,
    from_right,
    q_sum,
    ra2,
    from_left2,
    from_right2,
    z_send,
    wg,
    wu,
    wd,
    ain,
    cout,
    bq_got,
    e_got,
    pieces,
    pieces_got,
    joined,
    tx,
    t_ref,
    ct,
    bpad,
    epad,
    q_buf,
    cache,
    lens,
    ids,
    gates,
    att_buf,
    send_sem,
    recv_sem,
    local_sem,
):
    sect = lax.axis_index("sect")
    grp = lax.axis_index("grp")
    tp = lax.axis_index("tp")
    y = grp // 16
    zh = (grp // 4) % 4
    x = grp % 4
    z = zh * 2 + sect
    expert = grp // 4

    def plane(dy, dx):
        return (sect, ((y + dy) % 4) * 16 + zh * 4 + (x + dx) % 4, tp)

    def across(step):
        target = (z + step + 8) % 8
        return (target % 2, y * 16 + (target // 2) * 4 + x, tp)

    other_core = (sect, grp, 1 - tp)
    partner = (1 - sect, grp, tp)
    count = [0]

    def remote(src, dst, device):
        i = count[0]
        count[0] += 1
        return pltpu.make_async_remote_copy(
            src_ref=src,
            dst_ref=dst,
            send_sem=send_sem.at[i],
            recv_sem=recv_sem.at[i],
            device_id=device,
            device_id_type=MESH,
        )

    local_count = [0]

    def local(src, dst):
        i = local_count[0]
        local_count[0] += 1
        copy = pltpu.make_async_copy(src, dst, local_sem.at[i])
        copy.start()
        return copy

    barrier = pltpu.get_barrier_semaphore()
    peers = [other_core, plane(1, 0), plane(2, 0), plane(3, 0), plane(0, 1), plane(0, 3)]
    peers += [across(step) for step in STEPS]
    for peer in peers:
        pl.semaphore_signal(barrier, inc=1, device_id=peer, device_id_type=MESH)

    load_rows = local(rows_hbm.at[0], unit.at[:, pl.ds(0, HALF)])
    load_ids = local(ids_hbm.at[0], ids)
    load_gates = local(gates_hbm.at[0], gates)
    load_ain = local(ain_hbm.at[0, 0], ain)
    load_cout = local(cout_hbm.at[0, 0], cout)
    load_len = local(len_hbm, lens)
    load_q = local(q_hbm.at[0], q_buf)
    load_cache = local(cache_hbm.at[0], cache)
    load_wg = local(wg_hbm.at[0], wg)
    load_wu = local(wu_hbm.at[0], wu)
    load_wd = local(wd_hbm.at[0], wd)

    load_ids.wait()
    load_gates.wait()
    lane8 = lax.broadcasted_iota(jnp.int32, (SEQ, 128), 1)
    named = lane8 % 32
    share = jnp.zeros((SEQ, 128), F32)
    for k in range(8):
        share += jnp.where(ids[:, k : k + 1] == named, gates[:, k : k + 1], 0.0)
    first = share.astype(BF).astype(F32)
    second = (share - first).astype(BF).astype(F32)
    third = share - first - second
    terms = jnp.where(lane8 < 32, first, jnp.where(lane8 < 64, second, third))
    load_rows.wait()
    unit[:, HALF:WIDE] = jnp.where(lane8 < 96, terms, 0.0).astype(BF)

    pl.semaphore_wait(barrier, len(peers))

    z_copies = [
        remote(unit, zbuf.at[MIRROR[slot]], across(STEPS[slot])) for slot in range(4)
    ]
    for copy in z_copies:
        copy.start()
    bq_copy = remote(bq_hbm.at[0], bq_got, partner)
    e_copy = remote(e_hbm.at[0], e_got, partner)
    bq_copy.start()
    e_copy.start()

    load_ain.wait()
    load_cout.wait()
    lane56 = lax.broadcasted_iota(jnp.int32, (SLICE, 128), 1)

    def turned(tile, by):
        by = by % 128
        return tile if by == 0 else pltpu.roll(tile, by, 1)

    def piece(e, at):
        a_tile = ain[:, 128 * (e // 4) : 128 * (e // 4) + 128].astype(F32)
        c_tile = cout[:, 128 * (e // 8) : 128 * (e // 8) + 128].astype(F32)
        c_from = at - 16 * (e % 8)
        return jnp.where(
            lane56 < at + 32,
            turned(a_tile, at - 32 * (e % 4)),
            jnp.where(lane56 < at + 48, turned(c_tile, 32 + c_from), turned(c_tile, 48 + c_from)),
        )

    for i in range(4):
        for k in range(2):
            tile = jnp.where(lane56 < 64, piece(4 * i + k, 0), piece(4 * i + k + 2, 64))
            pieces[i, k] = tile.astype(BF)
    y_copies = [
        remote(
            pieces.at[(y + dy) % 4], pieces_got.at[y], plane(dy, 0)
        )
        for dy in (1, 3, 2)
    ]
    for copy in y_copies:
        copy.start()
    pieces_got[y] = pieces[y]

    def attend(first_seq, n):
        def one(s, carry):
            cached = cache[s]
            query = q_buf[s]
            scores = dot(query[:, :LAT], cached[:LAT]) + dot(query[:, LAT:], cached[LAT:])
            scores = scores * QK ** (-0.5)
            position = lax.broadcasted_iota(jnp.int32, (HEADS, LEN), 1)
            at = lax.broadcasted_iota(jnp.int32, (1, SEQ), 1) == s
            limit = jnp.sum(jnp.where(at, lens[...], 0), axis=1, keepdims=True)
            scores = jnp.where(position < limit, scores, -jnp.inf)
            top = jnp.max(scores, axis=1, keepdims=True)
            weights = jnp.exp(scores - top)
            probs = (weights / jnp.sum(weights, axis=1, keepdims=True)).astype(BF)
            att_buf[s] = dot_nt(probs, cached[:LAT]).astype(BF)
            return carry

        lax.fori_loop(first_seq, first_seq + n, one, 0)

    def rows_of(chain, du):
        return pl.ds(((0, 2, 3, 1)[du] * 2 + chain) * 16, 16)

    along = [
        dict(up=plane(0, 1), um=plane(0, 3), vp=plane(1, 0), vm=plane(3, 0)),
        dict(up=plane(1, 0), um=plane(3, 0), vp=plane(0, 1), vm=plane(0, 3)),
    ]
    left_x, right_x = pl.ds(0, QUARTER), pl.ds(QUARTER, WIDE - QUARTER)
    left, right = pl.ds(0, QUARTER), pl.ds(QUARTER, QUARTER)

    u_p, u_m, u_fp, u_fm = [], [], [], []
    v_p, v_m, v_fp, v_fm = [], [], [], []
    for c in range(2):
        d = along[c]
        own = x_ref.at[0, rows_of(c, 0)]
        u_p.append(remote(own, x_ref.at[0, rows_of(c, 3)], d["up"]))
        u_m.append(remote(own, x_ref.at[0, rows_of(c, 1)], d["um"]))
        u_fp.append(
            remote(
                x_ref.at[0, rows_of(c, 3), left_x], x_ref.at[0, rows_of(c, 2), left_x], d["up"]
            )
        )
        u_fm.append(
            remote(
                x_ref.at[0, rows_of(c, 1), right_x], x_ref.at[0, rows_of(c, 2), right_x], d["um"]
            )
        )
        v_p.append([])
        v_m.append([])
        v_fp.append([])
        v_fm.append([])
        for du in range(4):
            r = rows_of(c, du)
            v_p[c].append(remote(x_ref.at[0, r], x_ref.at[3, r], d["vp"]))
            v_m[c].append(remote(x_ref.at[0, r], x_ref.at[1, r], d["vm"]))
            v_fp[c].append(
                remote(x_ref.at[3, r, left_x], x_ref.at[2, r, left_x], d["vp"])
            )
            v_fm[c].append(
                remote(x_ref.at[1, r, right_x], x_ref.at[2, r, right_x], d["vm"])
            )

    def enter(c):
        for slot in CHAIN_SLOTS[c]:
            z_copies[MIRROR[slot]].wait_recv()
        a, b = CHAIN_SLOTS[c]
        x_ref[0, rows_of(c, 0)] = jnp.concatenate([zbuf[a], zbuf[b]], axis=0)
        u_p[c].start()
        u_m[c].start()
        v_p[c][0].start()
        v_m[c][0].start()

    def spread(c, du):
        v_p[c][du].start()
        v_m[c][du].start()

    def forward(c, du):
        v_p[c][du].wait_recv()
        v_fp[c][du].start()
        v_m[c][du].wait_recv()
        v_fm[c][du].start()

    def turn(c):
        u_p[c].wait_recv()
        u_fp[c].start()
        u_m[c].wait_recv()
        u_fm[c].start()
        spread(c, 3)

    def turn_far(c):
        u_fp[c].wait_recv()
        u_fm[c].wait_recv()
        spread(c, 2)

    enter(0)

    for copy in y_copies:
        copy.wait_recv()
    for k in range(4):
        for i in range(2):
            low = pieces_got[i, k % 2].astype(F32)
            high = pieces_got[i + 2, k % 2].astype(F32)
            if k < 2:
                high = pltpu.roll(high, 64, 1)
            else:
                low = pltpu.roll(low, 64, 1)
            joined[k, i] = jnp.where(lane56 < 64, low, high).astype(BF)
    t_copies = [
        remote(joined.at[((z + step + 8) % 8) // 2], tx.at[x, zh], across(step)) for step in STEPS
    ]
    for copy in t_copies:
        copy.start()

    enter(1)
    load_len.wait()
    load_q.wait()
    load_cache.wait()
    attend(0, 1)
    turn(0)
    forward(0, 0)

    for copy in t_copies:
        copy.wait_recv()
    before, after = (x + 3) % 4, (x + 1) % 4
    t_p = remote(tx.at[x], tx.at[x], plane(0, 1))
    t_m = remote(tx.at[x], tx.at[x], plane(0, 3))
    t_fp = remote(tx.at[before, pl.ds(0, 2)], tx.at[before, pl.ds(0, 2)], plane(0, 1))
    t_fm = remote(tx.at[after, pl.ds(2, 2)], tx.at[after, pl.ds(2, 2)], plane(0, 3))
    t_p.start()
    t_m.start()

    turn(1)
    spread(0, 1)
    spread(1, 1)
    forward(1, 0)

    bq_copy.wait_recv()
    e_copy.wait_recv()
    bpad[...] = jnp.zeros_like(bpad)
    bpad[0:16, 0:HID] = bq_got[0:16]
    bpad[16:32, HID : 2 * HID] = bq_got[16:32]
    epad[...] = jnp.zeros_like(epad)
    for at in (32, 48, 96, 112):
        epad[at : at + 16] = e_got[...]

    turn_far(0)
    turn_far(1)
    t_p.wait_recv()
    t_fp.start()
    t_m.wait_recv()
    t_fm.start()

    lane128 = lax.broadcasted_iota(jnp.int32, (128, 128), 1)
    low_at, gate_at, up_at = (
        pl.ds(2 * HID, 128),
        pl.ds(0, HID),
        pl.ds(HID, HID),
    )
    exchange = [
        [
            remote(gu_own.at[dv, :, at], gu_got.at[dv, :, at], other_core)
            for at in (gate_at, up_at, low_at)
        ]
        for dv in range(4)
    ]

    groups = (((0, 0, 128),), ((1, 0, 64), (3, 0, 64)), ((1, 64, 64), (3, 64, 64)), ((2, 0, 128),))

    def rows_in(g, lo, hi):
        parts = [x_ref[dv, at : at + n, lo:hi] for dv, at, n in groups[g]]
        return parts[0] if len(parts) == 1 else jnp.concatenate(parts, axis=0)

    def wide_product(g):
        gu_own[g, :, gate_at] = dot(rows_in(g, 0, HALF), wg[...])
        exchange[g][0].start()
        gu_own[g, :, up_at] = dot(rows_in(g, 0, HALF), wu[...])
        exchange[g][1].start()

    def low_product(g):
        low_a = dot(rows_in(g, 0, QUARTER), t_ref[...])
        low_b = dot(rows_in(g, QUARTER, HALF), t_ref[...])
        gu_own[g, :, low_at] = low_a + pltpu.roll(low_b, 64, 1)
        exchange[g][2].start()

    def second_product(g, after=None):
        exchange[g][2].wait_recv()
        low = (gu_own[g, :, low_at] + gu_got[g, :, low_at]).astype(BF)
        extra = dot(low, bpad[...])
        exchange[g][0].wait_recv()
        gate = gu_own[g, :, gate_at] + gu_got[g, :, gate_at] + extra[:, 0:HID]
        silu = gate / (1.0 + jnp.exp(-gate))
        exchange[g][1].wait_recv()
        up = gu_own[g, :, up_at] + gu_got[g, :, up_at] + extra[:, HID:]
        hidden = (silu * up).astype(BF)
        narrow = dot_nt(hidden, epad[...])
        head = narrow.astype(BF).astype(F32)
        rest = narrow - head
        split = jnp.where((lane128 % 64) < 48, head, rest)
        picks = (lane128 % 32 == expert) & (lane128 < 96)
        shares = rows_in(g, HALF, WIDE).astype(F32)
        share = jnp.sum(jnp.where(picks, shares, 0.0), axis=1, keepdims=True)
        for h in range(2):
            thin = jnp.where((lane128 // 64) == h, split, 0.0).astype(BF)
            for i in range(QUARTER // HID):
                at = i * HID
                there = h * QUARTER + at
                value = dot(hidden, wd[:, there : there + HID]) + dot(thin, ct[:, at : at + HID])
                value = (value * share).astype(BF)
                done = 0
                for dv, begin, n in groups[g]:
                    p_ref[dv, begin : begin + n, there : there + HID] = value[done : done + n]
                    done += n
            if after is not None:
                after(h)

    load_wg.wait()
    load_wu.wait()
    wide_product(0)
    forward(0, 3)
    forward(1, 3)
    wide_product(1)
    forward(0, 1)
    forward(1, 1)
    forward(0, 2)
    forward(1, 2)
    wide_product(2)

    t_fp.wait_recv()
    t_fm.wait_recv()
    for i in range(2):
        for k in range(4):
            block = jnp.concatenate([tx[j, k, i].astype(F32) for j in range(4)], axis=0)
            t_ref[224 * (4 * i + k) : 224 * (4 * i + k) + 224] = block.astype(BF)
    for k in range(14):
        block = t_ref[128 * k : 128 * k + 128].astype(F32)
        ct[:, 128 * k : 128 * k + 128] = block.T.astype(BF)
    low_product(1)
    low_product(2)
    load_wd.wait()
    second_product(1)

    a_p, a_m, b_p, b_m, c_p, c_m = [], [], [], [], [], []
    for c in range(2):
        d = along[c]
        for group in (a_p, a_m, b_p, b_m, c_p, c_m):
            group.append([])
        for du in range(4):
            r = rows_of(c, du)
            a_p[c].append(remote(p_ref.at[2, r, left], ra.at[0, r], d["vp"]))
            a_m[c].append(remote(p_ref.at[2, r, right], ra.at[1, r], d["vm"]))
            b_p[c].append(remote(p_ref.at[1, r, right], from_left.at[r, right], d["vp"]))
            b_m[c].append(remote(p_ref.at[3, r, left], from_right.at[r, left], d["vm"]))
            c_p[c].append(remote(p_ref.at[1, r, left], from_left.at[r, left], d["vp"]))
            c_m[c].append(remote(p_ref.at[3, r, right], from_right.at[r, right], d["vm"]))
    order = (2, 1, 3, 0)

    def direct(du):
        for c in range(2):
            b_p[c][du].start()
            b_m[c][du].start()

    direct(3)
    direct(0)
    second_product(2)
    direct(2)
    direct(1)
    for c in range(2):
        for du in range(4):
            v_fp[c][du].wait_recv()
            v_fm[c][du].wait_recv()
    low_product(3)
    wide_product(3)
    low_product(0)

    def begin_return(h):
        for du in order:
            for c in (1, 0):
                (a_p, a_m)[h][c][du].start()

    second_product(3, begin_return)
    second_product(0)
    attend(1, 7)
    store_att = local(att_buf, att_hbm.at[0])

    def carry_v(c, du):
        r = rows_of(c, du)
        a_p[c][du].wait_recv()
        p_ref[1, r, left] = (p_ref[1, r, left].astype(F32) + ra[0, r].astype(F32)).astype(BF)
        c_p[c][du].start()
        a_m[c][du].wait_recv()
        p_ref[3, r, right] = (p_ref[3, r, right].astype(F32) + ra[1, r].astype(F32)).astype(BF)
        c_m[c][du].start()

    def gather_v(c, du):
        r = rows_of(c, du)
        for copy in (b_p[c][du], c_p[c][du], b_m[c][du], c_m[c][du]):
            copy.wait_recv()
        total = p_ref[0, r].astype(F32) + from_left[r].astype(F32) + from_right[r].astype(F32)
        q_sum[r] = total.astype(BF)

    a2p, a2m, b2p, b2m, c2p, c2m = [], [], [], [], [], []
    for c in range(2):
        d = along[c]
        r1, r2, r3 = rows_of(c, 1), rows_of(c, 2), rows_of(c, 3)
        a2p.append(remote(q_sum.at[r2, left], ra2.at[0, c], d["up"]))
        a2m.append(remote(q_sum.at[r2, right], ra2.at[1, c], d["um"]))
        b2p.append(remote(q_sum.at[r1, right], from_left2.at[c, :, right], d["up"]))
        b2m.append(remote(q_sum.at[r3, left], from_right2.at[c, :, left], d["um"]))
        c2p.append(remote(q_sum.at[r1, left], from_left2.at[c, :, left], d["up"]))
        c2m.append(remote(q_sum.at[r3, right], from_right2.at[c, :, right], d["um"]))
    def turn_back(c):
        gather_v(c, 2)
        a2p[c].start()
        a2m[c].start()

    def near_back(c, du):
        gather_v(c, du)
        (b2p if du == 1 else b2m)[c].start()

    def carry_u(c):
        r1, r3 = rows_of(c, 1), rows_of(c, 3)
        a2p[c].wait_recv()
        q_sum[r1, left] = (q_sum[r1, left].astype(F32) + ra2[0, c].astype(F32)).astype(BF)
        c2p[c].start()
        a2m[c].wait_recv()
        q_sum[r3, right] = (q_sum[r3, right].astype(F32) + ra2[1, c].astype(F32)).astype(BF)
        c2m[c].start()

    z_back = [
        remote(z_send.at[slot], z_got.at[MIRROR[slot]], across(STEPS[slot])) for slot in range(4)
    ]

    def cross_back(c):
        for copy in (b2p[c], c2p[c], b2m[c], c2m[c]):
            copy.wait_recv()
        total = (
            q_sum[rows_of(c, 0)].astype(F32)
            + from_left2[c].astype(F32)
            + from_right2[c].astype(F32)
        )
        for i in range(2):
            slot = CHAIN_SLOTS[c][i]
            z_send[slot] = total[8 * i : 8 * i + 8].astype(BF)
            z_back[slot].start()

    carry_v(1, 2)
    carry_v(0, 2)
    carry_v(1, 1)
    carry_v(0, 1)
    turn_back(1)
    carry_v(1, 3)
    near_back(1, 1)
    carry_v(1, 0)
    near_back(1, 3)
    carry_v(0, 3)
    carry_u(1)
    carry_v(0, 0)
    turn_back(0)
    gather_v(1, 0)
    near_back(0, 1)
    near_back(0, 3)
    cross_back(1)
    carry_u(0)
    gather_v(0, 0)
    cross_back(0)

    for copy in z_copies + [bq_copy, e_copy] + y_copies + t_copies + [t_p, t_m, t_fp, t_fm]:
        copy.wait_send()
    for c in range(2):
        for copy in [u_p[c], u_m[c], u_fp[c], u_fm[c]] + v_p[c] + v_m[c] + v_fp[c] + v_fm[c]:
            copy.wait_send()
    for g in range(4):
        for copy in exchange[g]:
            copy.wait_send()

    for c in range(2):
        for group in (a_p, a_m, b_p, b_m, c_p, c_m):
            for copy in group[c]:
                copy.wait_send()
        for copy in (a2p[c], a2m[c], b2p[c], b2m[c], c2p[c], c2m[c]):
            copy.wait_send()
    store_att.wait()
    for copy in z_back:
        copy.wait_recv()
    for copy in z_back:
        copy.wait_send()
    assert count[0] == N_COPIES, count[0]


def finish(z_got, att_in, expert_hbm, att_hbm, parts, out_buf, att_buf, sems):
    load = pltpu.make_async_copy(z_got, parts, sems.at[0])
    load.start()
    load_att = pltpu.make_async_copy(att_in, att_buf, sems.at[1])
    load_att.start()
    load.wait()
    total = parts[0].astype(F32) + parts[1].astype(F32) + parts[2].astype(F32) + parts[3].astype(F32)
    out_buf[...] = total.astype(BF)
    store = pltpu.make_async_copy(out_buf, expert_hbm.at[0], sems.at[2])
    store.start()
    load_att.wait()
    store_att = pltpu.make_async_copy(att_buf, att_hbm, sems.at[3])
    store_att.start()
    store.wait()
    store_att.wait()


def body(
    queries,
    latent_rotary_cache,
    lengths,
    section_hidden_rows,
    row_expert_index,
    routing_gate_weight,
    gate_matrix,
    up_weight,
    down_weight,
    adapter_input_factor,
    adapter_output_factor,
    adapter_up_output,
    adapter_down_input,
):
    vmem = pltpu.VMEM
    returned, attended = pl.pallas_call(
        kernel,
        out_shape=(
            jax.ShapeDtypeStruct((4, SEQ, HALF), BF),
            jax.ShapeDtypeStruct((1, SEQ, HEADS, LAT), BF),
        ),
        in_specs=[pl.BlockSpec(memory_space=pl.ANY)] * 13,
        out_specs=[pl.BlockSpec(memory_space=pl.ANY)] * 2,
        scratch_shapes=[
            vmem((SEQ, WIDE), BF),
            vmem((4, SEQ, WIDE), BF),
            vmem((4, 128, WIDE), BF),
            vmem((4, 128, 2 * HID + 128), F32),
            vmem((4, 128, 2 * HID + 128), F32),
            vmem((4, 128, HALF), BF),
            vmem((2, 128, QUARTER), BF),
            vmem((128, HALF), BF),
            vmem((128, HALF), BF),
            vmem((128, HALF), BF),
            vmem((2, 2, 16, QUARTER), BF),
            vmem((2, 16, HALF), BF),
            vmem((2, 16, HALF), BF),
            vmem((4, SEQ, HALF), BF),
            vmem((HALF, HID), BF),
            vmem((HALF, HID), BF),
            vmem((HID, HALF), BF),
            vmem((SLICE, 512), BF),
            vmem((SLICE, 256), BF),
            vmem((32, HID), BF),
            vmem((16, HID), BF),
            vmem((4, 2, SLICE, 128), BF),
            vmem((4, 2, SLICE, 128), BF),
            vmem((4, 2, SLICE, 128), BF),
            vmem((4, 4, 2, SLICE, 128), BF),
            vmem((QUARTER, 128), BF),
            vmem((128, QUARTER), BF),
            vmem((128, 2 * HID), BF),
            vmem((128, HID), BF),
            vmem((SEQ, HEADS, KD), BF),
            vmem((SEQ, KD, LEN), BF),
            vmem((1, SEQ), jnp.int32),
            vmem((SEQ, 8), jnp.int32),
            vmem((SEQ, 8), F32),
            vmem((SEQ, HEADS, LAT), BF),
            pltpu.SemaphoreType.DMA((N_COPIES,)),
            pltpu.SemaphoreType.DMA((N_COPIES,)),
            pltpu.SemaphoreType.DMA((N_LOCAL,)),
        ],
        compiler_params=pltpu.CompilerParams(
            collective_id=0, has_side_effects=True, vmem_limit_bytes=56 * 1024 * 1024
        ),
    )(
        queries,
        jnp.swapaxes(latent_rotary_cache, 2, 3),
        lengths,
        section_hidden_rows,
        row_expert_index,
        routing_gate_weight,
        gate_matrix,
        up_weight,
        down_weight,
        adapter_input_factor,
        adapter_output_factor,
        adapter_up_output,
        adapter_down_input,
    )
    return pl.pallas_call(
        finish,
        out_shape=(
            jax.ShapeDtypeStruct((1, SEQ, HALF), BF),
            jax.ShapeDtypeStruct((1, SEQ, HEADS, LAT), BF),
        ),
        in_specs=[pl.BlockSpec(memory_space=pltpu.HBM)] * 2,
        out_specs=[pl.BlockSpec(memory_space=pltpu.HBM)] * 2,
        scratch_shapes=[
            vmem((4, SEQ, HALF), BF),
            vmem((SEQ, HALF), BF),
            vmem((1, SEQ, HEADS, LAT), BF),
            pltpu.SemaphoreType.DMA((4,)),
        ],
    )(returned, attended)


def solution(mesh):
    return jax.shard_map(
        body,
        mesh=mesh,
        in_specs=(
            P("sect", "grp", "tp", None),
            P("sect", "grp", None, None),
            P("sect", "grp"),
            P("sect", "grp", "tp"),
            P("sect", "grp", None),
            P("sect", "grp", None),
            P("sect", "tp", "grp"),
            P("sect", "tp", "grp"),
            P("sect", "grp", "tp"),
            P("sect", "tp", "grp", None),
            P("sect", "tp", "grp", None),
            P("sect", None, "grp"),
            P("sect", None, "grp"),
        ),
        out_specs=(P("sect", "grp", "tp"), P("sect", "grp", "tp", None)),
        check_vma=False,
    )
```

```python
import jax
import jax.numpy as jnp
from jax import lax
from jax.experimental import pallas as pl
from jax.experimental.pallas import tpu as pltpu
from jax.sharding import PartitionSpec as P

LAT = 512
QK = 192
SEQ = 8
HEADS = 64
KD = 576
LEN = 512
HALF = 3584
QUARTER = HALF // 2
WIDE = HALF + 128
HID = 256
SLICE = 56
N_COPIES = 133
N_LOCAL = 16
BF = jnp.bfloat16
F32 = jnp.float32
MESH = pl.DeviceIdType.MESH

STEPS = (1, -1, 3, -3)
MIRROR = (1, 0, 3, 2)
CHAIN_SLOTS = ((0, 1), (2, 3))


def dot(a, b):
    return jnp.dot(a, b, preferred_element_type=F32)


def dot_nt(a, b):
    return lax.dot_general(a, b, (((1,), (1,)), ((), ())), preferred_element_type=F32)


def kernel(
    q_hbm,
    cache_hbm,
    len_hbm,
    rows_hbm,
    ids_hbm,
    gates_hbm,
    wg_hbm,
    wu_hbm,
    wd_hbm,
    ain_hbm,
    cout_hbm,
    bq_hbm,
    e_hbm,
    z_got,
    att_hbm,
    unit,
    zbuf,
    x_ref,
    gu_own,
    gu_got,
    p_ref,
    ra,
    from_left,
    from_right,
    q_sum,
    ra2,
    from_left2,
    from_right2,
    z_send,
    wg,
    wu,
    wd,
    ain,
    cout,
    bq_got,
    e_got,
    pieces,
    pieces_got,
    joined,
    tx,
    t_ref,
    ct,
    bpad,
    epad,
    q_buf,
    cache,
    lens,
    ids,
    gates,
    att_buf,
    send_sem,
    recv_sem,
    local_sem,
):
    sect = lax.axis_index("sect")
    grp = lax.axis_index("grp")
    tp = lax.axis_index("tp")
    y = grp // 16
    zh = (grp // 4) % 4
    x = grp % 4
    z = zh * 2 + sect
    expert = grp // 4

    def plane(dy, dx):
        return (sect, ((y + dy) % 4) * 16 + zh * 4 + (x + dx) % 4, tp)

    def across(step):
        target = (z + step + 8) % 8
        return (target % 2, y * 16 + (target // 2) * 4 + x, tp)

    other_core = (sect, grp, 1 - tp)
    partner = (1 - sect, grp, tp)
    count = [0]

    def remote(src, dst, device):
        i = count[0]
        count[0] += 1
        return pltpu.make_async_remote_copy(
            src_ref=src,
            dst_ref=dst,
            send_sem=send_sem.at[i],
            recv_sem=recv_sem.at[i],
            device_id=device,
            device_id_type=MESH,
        )

    local_count = [0]

    def local(src, dst):
        i = local_count[0]
        local_count[0] += 1
        copy = pltpu.make_async_copy(src, dst, local_sem.at[i])
        copy.start()
        return copy

    barrier = pltpu.get_barrier_semaphore()
    peers = [other_core, plane(1, 0), plane(2, 0), plane(3, 0), plane(0, 1), plane(0, 3)]
    peers += [across(step) for step in STEPS]
    for peer in peers:
        pl.semaphore_signal(barrier, inc=1, device_id=peer, device_id_type=MESH)

    load_rows = local(rows_hbm.at[0], unit.at[:, pl.ds(0, HALF)])
    load_ids = local(ids_hbm.at[0], ids)
    load_gates = local(gates_hbm.at[0], gates)
    load_ain = local(ain_hbm.at[0, 0], ain)
    load_cout = local(cout_hbm.at[0, 0], cout)
    load_len = local(len_hbm, lens)
    load_q = local(q_hbm.at[0], q_buf)
    load_cache = local(cache_hbm.at[0], cache)
    load_wg = local(wg_hbm.at[0], wg)
    load_wu = local(wu_hbm.at[0], wu)
    load_wd = local(wd_hbm.at[0], wd)

    load_ids.wait()
    load_gates.wait()
    lane8 = lax.broadcasted_iota(jnp.int32, (SEQ, 128), 1)
    named = lane8 % 32
    share = jnp.zeros((SEQ, 128), F32)
    for k in range(8):
        share += jnp.where(ids[:, k : k + 1] == named, gates[:, k : k + 1], 0.0)
    first = share.astype(BF).astype(F32)
    second = (share - first).astype(BF).astype(F32)
    third = share - first - second
    terms = jnp.where(lane8 < 32, first, jnp.where(lane8 < 64, second, third))
    load_rows.wait()
    unit[:, HALF:WIDE] = jnp.where(lane8 < 96, terms, 0.0).astype(BF)

    pl.semaphore_wait(barrier, len(peers))

    z_copies = [
        remote(unit, zbuf.at[MIRROR[slot]], across(STEPS[slot])) for slot in range(4)
    ]
    z_copies[0].start()
    z_copies[1].start()
    bq_copy = remote(bq_hbm.at[0], bq_got, partner)
    e_copy = remote(e_hbm.at[0], e_got, partner)
    bq_copy.start()
    e_copy.start()

    load_ain.wait()
    load_cout.wait()
    lane56 = lax.broadcasted_iota(jnp.int32, (SLICE, 128), 1)

    def turned(tile, by):
        by = by % 128
        return tile if by == 0 else pltpu.roll(tile, by, 1)

    def piece(e, at):
        a_tile = ain[:, 128 * (e // 4) : 128 * (e // 4) + 128].astype(F32)
        c_tile = cout[:, 128 * (e // 8) : 128 * (e // 8) + 128].astype(F32)
        c_from = at - 16 * (e % 8)
        return jnp.where(
            lane56 < at + 32,
            turned(a_tile, at - 32 * (e % 4)),
            jnp.where(lane56 < at + 48, turned(c_tile, 32 + c_from), turned(c_tile, 48 + c_from)),
        )

    for i in range(4):
        for k in range(2):
            tile = jnp.where(lane56 < 64, piece(4 * i + k, 0), piece(4 * i + k + 2, 64))
            pieces[i, k] = tile.astype(BF)
    z_copies[2].start()
    z_copies[3].start()
    y_copies = [
        remote(
            pieces.at[(y + dy) % 4], pieces_got.at[y], plane(dy, 0)
        )
        for dy in (1, 3, 2)
    ]
    for copy in y_copies:
        copy.start()
    pieces_got[y] = pieces[y]

    def attend(first_seq, n):
        def one(s, carry):
            cached = cache[s]
            query = q_buf[s]
            scores = dot(query[:, :LAT], cached[:LAT]) + dot(query[:, LAT:], cached[LAT:])
            scores = scores * QK ** (-0.5)
            position = lax.broadcasted_iota(jnp.int32, (HEADS, LEN), 1)
            at = lax.broadcasted_iota(jnp.int32, (1, SEQ), 1) == s
            limit = jnp.sum(jnp.where(at, lens[...], 0), axis=1, keepdims=True)
            scores = jnp.where(position < limit, scores, -jnp.inf)
            top = jnp.max(scores, axis=1, keepdims=True)
            weights = jnp.exp(scores - top)
            probs = (weights / jnp.sum(weights, axis=1, keepdims=True)).astype(BF)
            att_buf[s] = dot_nt(probs, cached[:LAT]).astype(BF)
            return carry

        lax.fori_loop(first_seq, first_seq + n, one, 0)

    def rows_of(chain, du):
        return pl.ds(((0, 2, 3, 1)[du] * 2 + chain) * 16, 16)

    along = [
        dict(up=plane(0, 1), um=plane(0, 3), vp=plane(1, 0), vm=plane(3, 0)),
        dict(up=plane(1, 0), um=plane(3, 0), vp=plane(0, 1), vm=plane(0, 3)),
    ]
    left_x, right_x = pl.ds(0, QUARTER), pl.ds(QUARTER, WIDE - QUARTER)
    left, right = pl.ds(0, QUARTER), pl.ds(QUARTER, QUARTER)

    u_p, u_m, u_fp, u_fm = [], [], [], []
    v_p, v_m, v_fp, v_fm = [], [], [], []
    for c in range(2):
        d = along[c]
        own = x_ref.at[0, rows_of(c, 0)]
        u_p.append(remote(own, x_ref.at[0, rows_of(c, 3)], d["up"]))
        u_m.append(remote(own, x_ref.at[0, rows_of(c, 1)], d["um"]))
        u_fp.append(
            remote(
                x_ref.at[0, rows_of(c, 3), left_x], x_ref.at[0, rows_of(c, 2), left_x], d["up"]
            )
        )
        u_fm.append(
            remote(
                x_ref.at[0, rows_of(c, 1), right_x], x_ref.at[0, rows_of(c, 2), right_x], d["um"]
            )
        )
        v_p.append([])
        v_m.append([])
        v_fp.append([])
        v_fm.append([])
        for du in range(4):
            r = rows_of(c, du)
            v_p[c].append(remote(x_ref.at[0, r], x_ref.at[3, r], d["vp"]))
            v_m[c].append(remote(x_ref.at[0, r], x_ref.at[1, r], d["vm"]))
            v_fp[c].append(
                remote(x_ref.at[3, r, left_x], x_ref.at[2, r, left_x], d["vp"])
            )
            v_fm[c].append(
                remote(x_ref.at[1, r, right_x], x_ref.at[2, r, right_x], d["vm"])
            )

    def enter(c):
        for slot in CHAIN_SLOTS[c]:
            z_copies[MIRROR[slot]].wait_recv()
        a, b = CHAIN_SLOTS[c]
        x_ref[0, rows_of(c, 0)] = jnp.concatenate([zbuf[a], zbuf[b]], axis=0)
        u_p[c].start()
        u_m[c].start()
        v_p[c][0].start()
        v_m[c][0].start()

    def spread(c, du):
        v_p[c][du].start()
        v_m[c][du].start()

    def forward(c, du):
        v_p[c][du].wait_recv()
        v_fp[c][du].start()
        v_m[c][du].wait_recv()
        v_fm[c][du].start()

    def turn(c):
        u_p[c].wait_recv()
        u_fp[c].start()
        u_m[c].wait_recv()
        u_fm[c].start()
        spread(c, 3)

    def turn_far(c):
        u_fp[c].wait_recv()
        u_fm[c].wait_recv()
        spread(c, 2)

    enter(0)

    for copy in y_copies:
        copy.wait_recv()
    for k in range(4):
        for i in range(2):
            low = pieces_got[i, k % 2].astype(F32)
            high = pieces_got[i + 2, k % 2].astype(F32)
            if k < 2:
                high = pltpu.roll(high, 64, 1)
            else:
                low = pltpu.roll(low, 64, 1)
            joined[k, i] = jnp.where(lane56 < 64, low, high).astype(BF)
    t_copies = [
        remote(joined.at[((z + step + 8) % 8) // 2], tx.at[x, zh], across(step)) for step in STEPS
    ]
    for copy in t_copies:
        copy.start()

    enter(1)
    load_len.wait()
    load_q.wait()
    load_cache.wait()
    attend(0, 1)
    turn(0)
    forward(0, 0)

    for copy in t_copies:
        copy.wait_recv()
    before, after = (x + 3) % 4, (x + 1) % 4
    t_p = remote(tx.at[x], tx.at[x], plane(0, 1))
    t_m = remote(tx.at[x], tx.at[x], plane(0, 3))
    t_fp = remote(tx.at[before, pl.ds(0, 2)], tx.at[before, pl.ds(0, 2)], plane(0, 1))
    t_fm = remote(tx.at[after, pl.ds(2, 2)], tx.at[after, pl.ds(2, 2)], plane(0, 3))
    t_p.start()
    t_m.start()

    turn(1)
    spread(0, 1)
    spread(1, 1)
    forward(1, 0)

    bq_copy.wait_recv()
    e_copy.wait_recv()
    bpad[...] = jnp.zeros_like(bpad)
    bpad[0:16, 0:HID] = bq_got[0:16]
    bpad[16:32, HID : 2 * HID] = bq_got[16:32]
    epad[...] = jnp.zeros_like(epad)
    for at in (32, 48, 96, 112):
        epad[at : at + 16] = e_got[...]

    turn_far(0)
    turn_far(1)
    t_p.wait_recv()
    t_fp.start()
    t_m.wait_recv()
    t_fm.start()

    lane128 = lax.broadcasted_iota(jnp.int32, (128, 128), 1)
    low_at, gate_at, up_at = (
        pl.ds(2 * HID, 128),
        pl.ds(0, HID),
        pl.ds(HID, HID),
    )
    exchange = [
        [
            remote(gu_own.at[dv, :, at], gu_got.at[dv, :, at], other_core)
            for at in (gate_at, up_at, low_at)
        ]
        for dv in range(4)
    ]

    groups = (((0, 0, 128),), ((1, 0, 64), (3, 0, 64)), ((1, 64, 64), (3, 64, 64)), ((2, 0, 128),))

    def rows_in(g, lo, hi):
        parts = [x_ref[dv, at : at + n, lo:hi] for dv, at, n in groups[g]]
        return parts[0] if len(parts) == 1 else jnp.concatenate(parts, axis=0)

    def wide_product(g):
        gu_own[g, :, gate_at] = dot(rows_in(g, 0, HALF), wg[...])
        exchange[g][0].start()
        gu_own[g, :, up_at] = dot(rows_in(g, 0, HALF), wu[...])
        exchange[g][1].start()

    def low_product(g):
        low_a = dot(rows_in(g, 0, QUARTER), t_ref[...])
        low_b = dot(rows_in(g, QUARTER, HALF), t_ref[...])
        gu_own[g, :, low_at] = low_a + pltpu.roll(low_b, 64, 1)
        exchange[g][2].start()

    def second_product(g, after=None):
        exchange[g][2].wait_recv()
        low = (gu_own[g, :, low_at] + gu_got[g, :, low_at]).astype(BF)
        extra = dot(low, bpad[...])
        exchange[g][0].wait_recv()
        gate = gu_own[g, :, gate_at] + gu_got[g, :, gate_at] + extra[:, 0:HID]
        silu = gate / (1.0 + jnp.exp(-gate))
        exchange[g][1].wait_recv()
        up = gu_own[g, :, up_at] + gu_got[g, :, up_at] + extra[:, HID:]
        hidden = (silu * up).astype(BF)
        narrow = dot_nt(hidden, epad[...])
        head = narrow.astype(BF).astype(F32)
        rest = narrow - head
        split = jnp.where((lane128 % 64) < 48, head, rest)
        picks = (lane128 % 32 == expert) & (lane128 < 96)
        shares = rows_in(g, HALF, WIDE).astype(F32)
        share = jnp.sum(jnp.where(picks, shares, 0.0), axis=1, keepdims=True)
        for h in range(2):
            thin = jnp.where((lane128 // 64) == h, split, 0.0).astype(BF)
            for i in range(QUARTER // HID):
                at = i * HID
                there = h * QUARTER + at
                value = dot(hidden, wd[:, there : there + HID]) + dot(thin, ct[:, at : at + HID])
                value = (value * share).astype(BF)
                done = 0
                for dv, begin, n in groups[g]:
                    p_ref[dv, begin : begin + n, there : there + HID] = value[done : done + n]
                    done += n
            if after is not None:
                after(h)

    load_wg.wait()
    load_wu.wait()
    wide_product(0)
    forward(0, 3)
    forward(1, 3)
    wide_product(1)
    forward(0, 1)
    forward(1, 1)
    forward(0, 2)
    forward(1, 2)
    wide_product(2)

    t_fp.wait_recv()
    t_fm.wait_recv()
    for i in range(2):
        for k in range(4):
            block = jnp.concatenate([tx[j, k, i].astype(F32) for j in range(4)], axis=0)
            t_ref[224 * (4 * i + k) : 224 * (4 * i + k) + 224] = block.astype(BF)
    for k in range(14):
        block = t_ref[128 * k : 128 * k + 128].astype(F32)
        ct[:, 128 * k : 128 * k + 128] = block.T.astype(BF)
    low_product(1)
    low_product(2)
    load_wd.wait()
    second_product(1)

    a_p, a_m, b_p, b_m, c_p, c_m = [], [], [], [], [], []
    for c in range(2):
        d = along[c]
        for group in (a_p, a_m, b_p, b_m, c_p, c_m):
            group.append([])
        for du in range(4):
            r = rows_of(c, du)
            a_p[c].append(remote(p_ref.at[2, r, left], ra.at[0, r], d["vp"]))
            a_m[c].append(remote(p_ref.at[2, r, right], ra.at[1, r], d["vm"]))
            b_p[c].append(remote(p_ref.at[1, r, right], from_left.at[r, right], d["vp"]))
            b_m[c].append(remote(p_ref.at[3, r, left], from_right.at[r, left], d["vm"]))
            c_p[c].append(remote(p_ref.at[1, r, left], from_left.at[r, left], d["vp"]))
            c_m[c].append(remote(p_ref.at[3, r, right], from_right.at[r, right], d["vm"]))
    order = (2, 1, 3, 0)

    def direct(du):
        for c in range(2):
            b_p[c][du].start()
            b_m[c][du].start()

    direct(3)
    direct(0)
    second_product(2)
    direct(2)
    direct(1)
    for c in range(2):
        for du in range(4):
            v_fp[c][du].wait_recv()
            v_fm[c][du].wait_recv()
    low_product(3)
    wide_product(3)
    low_product(0)

    def begin_return(h):
        for du in order:
            for c in (1, 0):
                (a_p, a_m)[h][c][du].start()

    second_product(3, begin_return)
    second_product(0)
    attend(1, 7)
    store_att = local(att_buf, att_hbm.at[0])

    def carry_v(c, du):
        r = rows_of(c, du)
        a_p[c][du].wait_recv()
        p_ref[1, r, left] = (p_ref[1, r, left].astype(F32) + ra[0, r].astype(F32)).astype(BF)
        c_p[c][du].start()
        a_m[c][du].wait_recv()
        p_ref[3, r, right] = (p_ref[3, r, right].astype(F32) + ra[1, r].astype(F32)).astype(BF)
        c_m[c][du].start()

    def gather_v(c, du):
        r = rows_of(c, du)
        for copy in (b_p[c][du], c_p[c][du], b_m[c][du], c_m[c][du]):
            copy.wait_recv()
        total = p_ref[0, r].astype(F32) + from_left[r].astype(F32) + from_right[r].astype(F32)
        q_sum[r] = total.astype(BF)

    a2p, a2m, b2p, b2m, c2p, c2m = [], [], [], [], [], []
    for c in range(2):
        d = along[c]
        r1, r2, r3 = rows_of(c, 1), rows_of(c, 2), rows_of(c, 3)
        a2p.append(remote(q_sum.at[r2, left], ra2.at[0, c], d["up"]))
        a2m.append(remote(q_sum.at[r2, right], ra2.at[1, c], d["um"]))
        b2p.append(remote(q_sum.at[r1, right], from_left2.at[c, :, right], d["up"]))
        b2m.append(remote(q_sum.at[r3, left], from_right2.at[c, :, left], d["um"]))
        c2p.append(remote(q_sum.at[r1, left], from_left2.at[c, :, left], d["up"]))
        c2m.append(remote(q_sum.at[r3, right], from_right2.at[c, :, right], d["um"]))
    def turn_back(c):
        gather_v(c, 2)
        a2p[c].start()
        a2m[c].start()

    def near_back(c, du):
        gather_v(c, du)
        (b2p if du == 1 else b2m)[c].start()

    def carry_up(c):
        r1 = rows_of(c, 1)
        a2p[c].wait_recv()
        q_sum[r1, left] = (q_sum[r1, left].astype(F32) + ra2[0, c].astype(F32)).astype(BF)
        c2p[c].start()

    def carry_um(c):
        r3 = rows_of(c, 3)
        a2m[c].wait_recv()
        q_sum[r3, right] = (q_sum[r3, right].astype(F32) + ra2[1, c].astype(F32)).astype(BF)
        c2m[c].start()

    z_back = [
        remote(z_send.at[slot], z_got.at[MIRROR[slot]], across(STEPS[slot])) for slot in range(4)
    ]

    def cross_back(c):
        for copy in (b2p[c], c2p[c], b2m[c], c2m[c]):
            copy.wait_recv()
        total = (
            q_sum[rows_of(c, 0)].astype(F32)
            + from_left2[c].astype(F32)
            + from_right2[c].astype(F32)
        )
        for i in range(2):
            slot = CHAIN_SLOTS[c][i]
            z_send[slot] = total[8 * i : 8 * i + 8].astype(BF)
            z_back[slot].start()

    both = (1, 0)
    for du in (2, 1):
        for c in both:
            carry_v(c, du)
    for c in both:
        turn_back(c)
    for c in both:
        carry_v(c, 3)
    for c in both:
        near_back(c, 1)
    for c in both:
        carry_v(c, 0)
    for c in both:
        carry_up(c)
    for c in both:
        near_back(c, 3)
        carry_um(c)
    for c in both:
        gather_v(c, 0)
    for c in both:
        cross_back(c)

    for copy in z_copies + [bq_copy, e_copy] + y_copies + t_copies + [t_p, t_m, t_fp, t_fm]:
        copy.wait_send()
    for c in range(2):
        for copy in [u_p[c], u_m[c], u_fp[c], u_fm[c]] + v_p[c] + v_m[c] + v_fp[c] + v_fm[c]:
            copy.wait_send()
    for g in range(4):
        for copy in exchange[g]:
            copy.wait_send()

    for c in range(2):
        for group in (a_p, a_m, b_p, b_m, c_p, c_m):
            for copy in group[c]:
                copy.wait_send()
        for copy in (a2p[c], a2m[c], b2p[c], b2m[c], c2p[c], c2m[c]):
            copy.wait_send()
    store_att.wait()
    for copy in z_back:
        copy.wait_recv()
    for copy in z_back:
        copy.wait_send()
    assert count[0] == N_COPIES, count[0]


def finish(z_got, att_in, expert_hbm, att_hbm, parts, out_buf, att_buf, sems):
    load = pltpu.make_async_copy(z_got, parts, sems.at[0])
    load.start()
    load_att = pltpu.make_async_copy(att_in, att_buf, sems.at[1])
    load_att.start()
    load.wait()
    total = parts[0].astype(F32) + parts[1].astype(F32) + parts[2].astype(F32) + parts[3].astype(F32)
    out_buf[...] = total.astype(BF)
    store = pltpu.make_async_copy(out_buf, expert_hbm.at[0], sems.at[2])
    store.start()
    load_att.wait()
    store_att = pltpu.make_async_copy(att_buf, att_hbm, sems.at[3])
    store_att.start()
    store.wait()
    store_att.wait()


def body(
    queries,
    latent_rotary_cache,
    lengths,
    section_hidden_rows,
    row_expert_index,
    routing_gate_weight,
    gate_matrix,
    up_weight,
    down_weight,
    adapter_input_factor,
    adapter_output_factor,
    adapter_up_output,
    adapter_down_input,
):
    vmem = pltpu.VMEM
    returned, attended = pl.pallas_call(
        kernel,
        out_shape=(
            jax.ShapeDtypeStruct((4, SEQ, HALF), BF),
            jax.ShapeDtypeStruct((1, SEQ, HEADS, LAT), BF),
        ),
        in_specs=[pl.BlockSpec(memory_space=pl.ANY)] * 13,
        out_specs=[pl.BlockSpec(memory_space=pl.ANY)] * 2,
        scratch_shapes=[
            vmem((SEQ, WIDE), BF),
            vmem((4, SEQ, WIDE), BF),
            vmem((4, 128, WIDE), BF),
            vmem((4, 128, 2 * HID + 128), F32),
            vmem((4, 128, 2 * HID + 128), F32),
            vmem((4, 128, HALF), BF),
            vmem((2, 128, QUARTER), BF),
            vmem((128, HALF), BF),
            vmem((128, HALF), BF),
            vmem((128, HALF), BF),
            vmem((2, 2, 16, QUARTER), BF),
            vmem((2, 16, HALF), BF),
            vmem((2, 16, HALF), BF),
            vmem((4, SEQ, HALF), BF),
            vmem((HALF, HID), BF),
            vmem((HALF, HID), BF),
            vmem((HID, HALF), BF),
            vmem((SLICE, 512), BF),
            vmem((SLICE, 256), BF),
            vmem((32, HID), BF),
            vmem((16, HID), BF),
            vmem((4, 2, SLICE, 128), BF),
            vmem((4, 2, SLICE, 128), BF),
            vmem((4, 2, SLICE, 128), BF),
            vmem((4, 4, 2, SLICE, 128), BF),
            vmem((QUARTER, 128), BF),
            vmem((128, QUARTER), BF),
            vmem((128, 2 * HID), BF),
            vmem((128, HID), BF),
            vmem((SEQ, HEADS, KD), BF),
            vmem((SEQ, KD, LEN), BF),
            vmem((1, SEQ), jnp.int32),
            vmem((SEQ, 8), jnp.int32),
            vmem((SEQ, 8), F32),
            vmem((SEQ, HEADS, LAT), BF),
            pltpu.SemaphoreType.DMA((N_COPIES,)),
            pltpu.SemaphoreType.DMA((N_COPIES,)),
            pltpu.SemaphoreType.DMA((N_LOCAL,)),
        ],
        compiler_params=pltpu.CompilerParams(
            collective_id=0, has_side_effects=True, vmem_limit_bytes=56 * 1024 * 1024
        ),
    )(
        queries,
        jnp.swapaxes(latent_rotary_cache, 2, 3),
        lengths,
        section_hidden_rows,
        row_expert_index,
        routing_gate_weight,
        gate_matrix,
        up_weight,
        down_weight,
        adapter_input_factor,
        adapter_output_factor,
        adapter_up_output,
        adapter_down_input,
    )
    return pl.pallas_call(
        finish,
        out_shape=(
            jax.ShapeDtypeStruct((1, SEQ, HALF), BF),
            jax.ShapeDtypeStruct((1, SEQ, HEADS, LAT), BF),
        ),
        in_specs=[pl.BlockSpec(memory_space=pltpu.HBM)] * 2,
        out_specs=[pl.BlockSpec(memory_space=pltpu.HBM)] * 2,
        scratch_shapes=[
            vmem((4, SEQ, HALF), BF),
            vmem((SEQ, HALF), BF),
            vmem((1, SEQ, HEADS, LAT), BF),
            pltpu.SemaphoreType.DMA((4,)),
        ],
    )(returned, attended)


def solution(mesh):
    return jax.shard_map(
        body,
        mesh=mesh,
        in_specs=(
            P("sect", "grp", "tp", None),
            P("sect", "grp", None, None),
            P("sect", "grp"),
            P("sect", "grp", "tp"),
            P("sect", "grp", None),
            P("sect", "grp", None),
            P("sect", "tp", "grp"),
            P("sect", "tp", "grp"),
            P("sect", "grp", "tp"),
            P("sect", "tp", "grp", None),
            P("sect", "tp", "grp", None),
            P("sect", None, "grp"),
            P("sect", None, "grp"),
        ),
        out_specs=(P("sect", "grp", "tp"), P("sect", "grp", "tp", None)),
        check_vma=False,
    )
```
